256 devices in a mesh: dp: 32 (over x, z_lo, y), tensor: 8 (over z_hi, core).
Axes of the slice: x: 4, y: 4, z: 8 (z_hi: 4, z_lo: 2; z = z_hi * 2 + z_lo), core: 2. Of those that a mesh axis runs over, the one named last changes fastest.
Arguments:
- hidden_input_rows: bfloat16 [4096, 8192], P('dp'), may hold values from -6 to 6
- output_gradient: bfloat16 [4096, 8192], P('dp', 'tensor'), may hold values from -6 to 6
- gate_activation: bfloat16 [4096, 28672], P(None, ('dp', 'tensor')), may hold values from -0.25 to 2.5
- down_projection_codes: int32 [28672, 8192], P('dp', 'tensor'), may hold values from 0 to 15
- block_scale_codes: int32 [448, 8192], P('dp', 'tensor'), may hold values from 0 to 255
- outer_level_scales: float32 [448, 128], P('dp', 'tensor'), may hold values from 0.03 to 0.08
- adapter_down_factor: bfloat16 [16, 8192], replicated, may hold values from -0.0625 to 0.0625
- adapter_up_factor: bfloat16 [16, 28672], P(None, 'dp'), may hold values from -0.03125 to 0.03125
- query_down_gradient: bfloat16 [128, 16, 8192], P('dp', None, 'tensor'), may hold values from -0.0014648438 to 0.0014648438
- query_up_gradient: bfloat16 [128, 16, 28672], P(None, None, ('dp', 'tensor')), may hold values from -0.0007324219 to 0.0007324219
Outputs:
- scores: float32 [32, 128], P('dp', 'tensor')
The draws below stay inside these ranges and needn't reach their ends.
Inputs may be any that keep to these rules, and one draw needn't show every extreme that they name: `down_projection_codes`: index into the sixteen NF4 levels. `block_scale_codes`: 8-bit scale code.
All inputs are finite; a program needn't handle non-finite values.
Results may differ from the reference program's by a relative error of at most 0.014.
Values may be sent and summed in bfloat16 or wider, within the bound.
A program may use at most 128 MiB of HBM per device.

```python
import math
import jax
import jax.numpy as jnp
from jax import lax

MODEL_WIDTH = 8192
HIDDEN_UNITS = 28672
ADAPTER_RANK = 16
BLOCK = 64
GROUP = 64
SEQ = 128
TOKENS = 4096
QUERIES = 128


def place_ends(values, rng, least, largest):
    shape = values.shape
    place = [jax.random.randint(jax.random.fold_in(rng, axis), (), 0, shape[axis]) for axis in range(len(shape))]
    values = values.at[tuple(place)].set(least)
    longest = shape.index(max(shape))
    place[longest] = (place[longest] + 1) % shape[longest]
    return values.at[tuple(place)].set(largest)


def shard_levels(own_key, extent, pieces, smallest, top_value):
    def one(dim, parts):
        heights = jax.random.uniform(jax.random.fold_in(jax.random.fold_in(own_key, 6), dim), (parts,), jnp.float32, smallest / len(pieces), top_value / len(pieces))
        return jnp.repeat(jnp.exp(heights), extent[dim] // parts).reshape((-1,) + (1,) * (len(extent) - dim - 1))

    factor_of = one(*pieces[0])
    for cut in pieces[1:]:
        factor_of = factor_of * one(*cut)
    return factor_of


def centred(key, extent, spread, most, split=(), kind=jnp.bfloat16):
    array = spread * jax.random.normal(key, extent, jnp.float32)
    if split:
        array = array * shard_levels(key, extent, split, -0.22, 0.18)
    return jnp.clip(array, -most, most).astype(kind)


def setup_inputs(seed: int = 0) -> dict:
    seeds = jax.random.split(jax.random.key(seed), 11)
    hidden_input_rows = centred(seeds[0], (TOKENS, MODEL_WIDTH), 1.0, 6.0, ((0, 32),))
    output_gradient = centred(seeds[1], (TOKENS, MODEL_WIDTH), 1.0, 6.0, ((0, 32), (1, 8)))
    gate_activation = jnp.clip(-0.25 + 2.75 * jax.random.uniform(seeds[2], (TOKENS, HIDDEN_UNITS), jnp.float32) ** shard_levels(seeds[2], (TOKENS, HIDDEN_UNITS), ((1, 256),), -0.2, 0.2), -0.25, 2.5).astype(jnp.bfloat16)
    down_projection_codes = place_ends(jax.random.randint(seeds[3], (HIDDEN_UNITS, MODEL_WIDTH), 0, 16), jax.random.fold_in(seeds[3], 1), 0, 15).astype(jnp.int32)
    block_scale_codes = place_ends(jax.random.randint(seeds[4], (HIDDEN_UNITS // BLOCK, MODEL_WIDTH), 0, 256), jax.random.fold_in(seeds[4], 1), 0, 255).astype(jnp.int32)
    outer_level_scales = jnp.clip(jnp.exp(math.log(0.08) - 0.98082925 * jax.random.uniform(seeds[5], (HIDDEN_UNITS // BLOCK, MODEL_WIDTH // GROUP), jnp.float32) ** shard_levels(seeds[5], (HIDDEN_UNITS // BLOCK, MODEL_WIDTH // GROUP), ((0, 32), (1, 8)), -0.2, 0.2)), 0.03, 0.08)
    adapter_down_factor = centred(seeds[6], (ADAPTER_RANK, MODEL_WIDTH), MODEL_WIDTH ** -0.5, 0.0625)
    adapter_up_factor = centred(seeds[7], (ADAPTER_RANK, HIDDEN_UNITS), HIDDEN_UNITS ** -0.5, 0.03125, ((1, 32),))
    query_down_gradient = centred(seeds[8], (QUERIES, ADAPTER_RANK, MODEL_WIDTH), (MODEL_WIDTH * ADAPTER_RANK * SEQ) ** -0.5, 0.0014648438, ((0, 32), (2, 8)))
    query_up_gradient = centred(seeds[9], (QUERIES, ADAPTER_RANK, HIDDEN_UNITS), (HIDDEN_UNITS * ADAPTER_RANK * SEQ) ** -0.5, 0.0007324219, ((2, 256),))
    return dict(hidden_input_rows=hidden_input_rows, output_gradient=output_gradient, gate_activation=gate_activation, down_projection_codes=down_projection_codes, block_scale_codes=block_scale_codes, outer_level_scales=outer_level_scales, adapter_down_factor=adapter_down_factor, adapter_up_factor=adapter_up_factor, query_down_gradient=query_down_gradient, query_up_gradient=query_up_gradient)


levels = (-1.0, -0.6961928009986877, -0.5250730514526367, -0.39491748809814453,
          -0.28444138169288635, -0.18477343022823334, -0.09105003625154495, 0.0,
          0.07958029955625534, 0.16093020141124725, 0.24611230194568634, 0.33791524171829224,
          0.44070982933044434, 0.5626170039176941, 0.7229568362236023, 1.0)


def dequantize(codes, block_codes, second_scales):
    values = jnp.zeros(codes.shape, jnp.float32)
    for level_index in range(16):
        values = jnp.where(codes == level_index, jnp.float32(levels[level_index]), values)
    column_scale = jnp.repeat(second_scales, GROUP, axis=1)
    scaling = (block_codes + 1).astype(jnp.float32) / 256.0 * column_scale
    row_count = codes.shape[0]
    col_count = codes.shape[1]
    values = values.reshape(row_count // BLOCK, BLOCK, col_count) * scaling[:, None, :]
    return values.reshape(row_count, col_count).astype(jnp.bfloat16)


def reference(hidden_input_rows, output_gradient, gate_activation, down_projection_codes, block_scale_codes, outer_level_scales, adapter_down_factor, adapter_up_factor, query_down_gradient, query_up_gradient):
    highest = lax.Precision.HIGHEST
    tokens_all = hidden_input_rows.shape[0]
    examples = tokens_all // SEQ
    projected_rows = jnp.dot(hidden_input_rows, adapter_down_factor.T, preferred_element_type=jnp.float32).astype(jnp.bfloat16)
    proj_wide = projected_rows.astype(jnp.float32).reshape(examples, SEQ, ADAPTER_RANK)
    cot_wide = output_gradient.astype(jnp.float32)
    piece_count = 8
    slice_width = HIDDEN_UNITS // piece_count

    def one_piece(index, carry):
        score_b, factors = carry
        start_offset = (index * slice_width).astype(jnp.int32)
        codes = lax.dynamic_slice_in_dim(down_projection_codes, start_offset, slice_width, 0)
        block_start = (index * (slice_width // BLOCK)).astype(jnp.int32)
        block_codes = lax.dynamic_slice_in_dim(block_scale_codes, block_start, slice_width // BLOCK, 0)
        second_scales = lax.dynamic_slice_in_dim(outer_level_scales, block_start, slice_width // BLOCK, 0)
        weights = dequantize(codes, block_codes, second_scales).astype(jnp.float32)
        hidden_grad = jnp.dot(cot_wide, weights.T, precision=highest)
        gate_piece = lax.dynamic_slice_in_dim(gate_activation, start_offset, slice_width, 1).astype(jnp.float32)
        upward = hidden_grad * gate_piece
        grad_b = jnp.einsum("esr,esf->erf", proj_wide, upward.reshape(examples, SEQ, slice_width),
                            precision=highest).astype(jnp.bfloat16)
        query_piece = lax.dynamic_slice_in_dim(query_up_gradient, start_offset, slice_width, 2).astype(jnp.float32)
        score_b = score_b + jnp.einsum("erf,qrf->eq", grad_b.astype(jnp.float32), query_piece, precision=highest)
        factor_portion = lax.dynamic_slice_in_dim(adapter_up_factor, start_offset, slice_width, 1).astype(jnp.float32)
        factors = factors + jnp.dot(upward, factor_portion.T, precision=highest)
        return score_b, factors

    initial = (jnp.zeros((examples, QUERIES), jnp.float32), jnp.zeros((tokens_all, ADAPTER_RANK), jnp.float32))
    score_b, factors = lax.fori_loop(0, piece_count, one_piece, initial)
    grad_a = jnp.einsum("esr,esd->erd", factors.reshape(examples, SEQ, ADAPTER_RANK),
                        hidden_input_rows.astype(jnp.float32).reshape(examples, SEQ, MODEL_WIDTH),
                        precision=highest).astype(jnp.bfloat16)
    score_a = jnp.einsum("erd,qrd->eq", grad_a.astype(jnp.float32), query_down_gradient.astype(jnp.float32), precision=highest)
    return score_a + score_b
```

```python
import jax
import jax.numpy as jnp
from jax import lax
from jax.experimental import pallas as pl
from jax.experimental.pallas import tpu as pltpu
from jax.sharding import PartitionSpec as P

MESH = pl.DeviceIdType.MESH
F32 = jnp.float32
BF16 = jnp.bfloat16
NT = (((1,), (1,)), ((), ()))
NN = (((1,), (0,)), ((), ()))
ANY = pl.BlockSpec(memory_space=pl.ANY)

PIECES = 16
SLOTS = 8
STAGES = 4

LEVELS = (
    -1.0,
    -0.6961928009986877,
    -0.5250730514526367,
    -0.39491748809814453,
    -0.28444138169288635,
    -0.18477343022823334,
    -0.09105003625154495,
    0.0,
    0.07958029955625534,
    0.16093020141124725,
    0.24611230194568634,
    0.33791524171829224,
    0.44070982933044434,
    0.5626170039176941,
    0.7229568362236023,
    1.0,
)


def lookup(codes):
    values = [jnp.full(codes.shape, level, F32) for level in LEVELS]
    for bit in range(4):
        odd = (codes & (1 << bit)) != 0
        values = [jnp.where(odd, values[i + 1], values[i]) for i in range(0, len(values), 2)]
    return values[0]


def offset(k):
    return k + k // 2 - 2 * (k // 3)


def piece_uv(n):
    late = jnp.maximum(n - 4, 0)
    first = n < 4
    return jnp.where(first, n, late // 3), jnp.where(first, 0, 1 + late % 3)


def kernel(
    x_hbm, og_hbm, gate_hbm, codes_hbm, bsc_hbm, osc_hbm, ad_hbm, au_hbm, qd_hbm, qu_hbm,
    out_ref,
    buf, qbuf, codes, bsc, osc, scale, w, xs, ad, au, auj, gate, qu, qf, qt,
    prod, own, csend, crecv, rsend, rrecv, proj, gb, fac, t1, t2s, t2, mt, acc, t3s, t3,
    lsem, og_ss, og_rs, qd_ss, qd_rs, c_ss, c_rs, r_ss, r_rs, p_ss, p_rs, t1_ss, t1_rs, t2_ss, t2_rs, t3_ss, t3_rs,
):
    dp = lax.axis_index("dp")
    tn = lax.axis_index("tensor")
    y, l, x = dp % 4, (dp // 4) % 2, dp // 8
    zh, c = tn // 2, tn % 2

    width = og_hbm.shape[1]
    here = x * 4 + y
    loads = [
        (og_hbm.at[pl.ds(0, 64)], buf.at[0, here, l]),
        (og_hbm.at[pl.ds(64, 64)], buf.at[1, here, l]),
        (codes_hbm, codes),
        (bsc_hbm, bsc),
        (osc_hbm, osc),
        (x_hbm, xs),
        (ad_hbm, ad),
        (au_hbm, au),
        (gate_hbm, gate),
        (qd_hbm.at[pl.ds(0, 32)], qbuf.at[0, here, l]),
        (qd_hbm.at[pl.ds(32, 32)], qbuf.at[1, here, l]),
        (qu_hbm, qu),
    ]
    loads = [pltpu.make_async_copy(a, b, lsem.at[i]) for i, (a, b) in enumerate(loads)]
    for load in loads:
        load.start()

    barrier = pltpu.get_barrier_semaphore()

    def greet_dp(o, _):
        pl.semaphore_signal(barrier, 1, device_id={"dp": (dp + o) % 32}, device_id_type=MESH)
        return 0

    def greet_tn(o, _):
        pl.semaphore_signal(barrier, 1, device_id={"tensor": (tn + o) % 8}, device_id_type=MESH)
        return 0

    lax.fori_loop(1, 32, greet_dp, 0)
    lax.fori_loop(1, 8, greet_tn, 0)
    pl.semaphore_wait(barrier, 38)

    def pair_at(k, u, v):
        a, b = offset(u), offset(v)
        if k == 0:
            return ((x + a) % 4) * 4 + (y + b) % 4
        return ((x + b) % 4) * 4 + (y + a) % 4

    def near(k, first, step):
        along_x = first == (k == 0)
        if along_x:
            return {"dp": (((x + step) % 4) * 2 + l) * 4 + y}
        return {"dp": (x * 2 + l) * 4 + (y + step) % 4}

    def piece_copy(data, ss, rs, k, u, v, half, ur, vr, target):
        ref = data.at[k, pair_at(k, u, v), half]
        return pltpu.make_async_remote_copy(
            src_ref=ref, dst_ref=ref, send_sem=ss.at[k, ur, vr, half], recv_sem=rs.at[k, ur, vr, half],
            device_id=target, device_id_type=MESH,
        )

    partner = {"dp": (x * 2 + 1 - l) * 4 + y}

    def gather_start(data, ss, rs):
        for k in range(2):
            piece_copy(data, ss, rs, k, 0, 0, l, 0, 0, partner).start()
            piece_copy(data, ss, rs, k, 0, 0, l, 2, 0, near(k, True, 1)).start()
            piece_copy(data, ss, rs, k, 0, 0, l, 1, 0, near(k, True, 3)).start()

    def gather_second(data, ss, rs, u):
        for k in range(2):
            for half in range(2):
                piece_copy(data, ss, rs, k, u, 0, half, u, 2, near(k, False, 1)).start()
                piece_copy(data, ss, rs, k, u, 0, half, u, 1, near(k, False, 3)).start()

    def gather_step(data, ss, rs, n):
        u, v = piece_uv(n)

        @pl.when(n == 0)
        def _():
            for k in range(2):
                piece_copy(data, ss, rs, k, 0, 0, 1 - l, 0, 0, partner).wait_recv()
                piece_copy(data, ss, rs, k, 0, 0, 1 - l, 2, 0, near(k, True, 1)).start()
                piece_copy(data, ss, rs, k, 0, 0, 1 - l, 1, 0, near(k, True, 3)).start()

        @pl.when(n > 0)
        def _():
            for k in range(2):
                for half in range(2):
                    piece_copy(data, ss, rs, k, u, v, half, u, v, partner).wait_recv()

        @pl.when(n == 1)
        def _():
            for k in range(2):
                piece_copy(data, ss, rs, k, 1, 0, 1, 3, 0, near(k, True, 3)).start()

        @pl.when(n == 2)
        def _():
            for k in range(2):
                piece_copy(data, ss, rs, k, 2, 0, 0, 3, 0, near(k, True, 1)).start()

        @pl.when(v == 1)
        def _():
            for k in range(2):
                piece_copy(data, ss, rs, k, u, 1, 1, u, 3, near(k, False, 3)).start()

        @pl.when(v == 2)
        def _():
            for k in range(2):
                piece_copy(data, ss, rs, k, u, 2, 0, u, 3, near(k, False, 1)).start()

        nxt = jnp.where(n == 1, 0, jnp.where(n == 3, 1, jnp.where(n == 4, 2, 3)))

        @pl.when((n == 1) | (n == 3) | (n == 4) | (n == 7))
        def _():
            gather_second(data, ss, rs, nxt)

    def gather_drain(data, ss, rs):
        def body(i, _):
            u, v = i // 4, i % 4
            for k in range(2):
                for half in range(2):
                    piece_copy(data, ss, rs, k, 0, 0, half, u, v, partner).wait_send()
            return 0

        for k in range(2):
            piece_copy(data, ss, rs, k, 0, 0, l, 0, 0, partner).wait_send()
        lax.fori_loop(1, 16, body, 0)

    og = (buf, og_ss, og_rs)
    qd = (qbuf, qd_ss, qd_rs)

    loads[0].wait()
    loads[1].wait()
    gather_start(*og)

    loads[5].wait()
    loads[6].wait()
    proj[dp] = lax.dot_general(ad[...], xs[...], NT, preferred_element_type=F32).astype(BF16)

    def proj_copy(o, to):
        return pltpu.make_async_remote_copy(
            src_ref=proj.at[dp], dst_ref=proj.at[dp], send_sem=p_ss.at[o], recv_sem=p_rs.at[o],
            device_id={"dp": (dp + o) % 32}, device_id_type=MESH,
        )

    def proj_send(o, _):
        proj_copy(o, None).start()
        return 0

    lax.fori_loop(1, 32, proj_send, 0)

    loads[3].wait()
    loads[4].wait()
    lane14 = lax.broadcasted_iota(jnp.int32, (14, 128), 1)
    for col in range(width // 128):
        pick = jnp.where(
            lane14 < 64,
            jnp.broadcast_to(osc[:, 2 * col : 2 * col + 1], (14, 128)),
            jnp.broadcast_to(osc[:, 2 * col + 1 : 2 * col + 2], (14, 128)),
        )
        at = pl.ds(col * 128, 128)
        scale[:, at] = (bsc[:, at] + 1).astype(F32) / 256.0 * pick
    loads[2].wait()

    def dequant(b, _):
        rows = pl.ds(pl.multiple_of(b * 64, 64), 64)
        w[rows, :] = (lookup(codes[rows, :]) * scale[pl.ds(b, 1), :]).astype(BF16)
        return 0

    lax.fori_loop(0, 14, dequant, 0)

    loads[7].wait()
    mine = jnp.zeros((16, 112), F32)
    for j in range(8):
        mine = jnp.where(tn == j, au[:, j * 112 : (j + 1) * 112].astype(F32), mine)
    auj[...] = mine.astype(BF16)
    gb[...] = jnp.zeros_like(gb)
    fac[...] = jnp.zeros_like(fac)
    loads[8].wait()

    def core_copy(p):
        return pltpu.make_async_remote_copy(
            src_ref=csend.at[p], dst_ref=crecv.at[p], send_sem=c_ss.at[p], recv_sem=c_rs.at[p],
            device_id={"tensor": zh * 2 + 1 - c}, device_id_type=MESH,
        )

    def ring_copy(p, d, i):
        step = 1 if d == 0 else 3
        return pltpu.make_async_remote_copy(
            src_ref=rsend.at[p, d, i], dst_ref=rrecv.at[p, d, i], send_sem=r_ss.at[p, d, i],
            recv_sem=r_rs.at[p, d, i],
            device_id={"tensor": ((zh + step) % 4) * 2 + c}, device_id_type=MESH,
        )

    def ring_target(d, i):
        return (zh + (3 - i if d == 0 else i + 1)) % 4

    def multiply(p):
        u, v = piece_uv(p)
        rows = jnp.concatenate(
            [buf[0, pair_at(0, u, v)].reshape(128, width), buf[1, pair_at(1, u, v)].reshape(128, width)], axis=0
        )
        prod[...] = lax.dot_general(w[...], rows, NT, preferred_element_type=F32).reshape(8, 112, 256)
        slot = p % SLOTS
        for k in range(4):
            csend[p, k] = prod[2 * k + 1 - c].astype(BF16)
            own[slot, k] = prod[2 * k + c]
        core_copy(p).start()

    def core_add(p):
        core_copy(p).wait_recv()
        slot = p % SLOTS
        for k in range(4):
            own[slot, k] += crecv[p, k].astype(F32)
        for d in range(2):
            rsend[p, d, 0] = own[slot, ring_target(d, 0), :, d * 128 : (d + 1) * 128].astype(BF16)
            ring_copy(p, d, 0).start()

    def ring_add(p, i):
        slot = p % SLOTS
        for d in range(2):
            ring_copy(p, d, i - 1).wait_recv()
            part = own[slot, ring_target(d, i), :, d * 128 : (d + 1) * 128]
            rsend[p, d, i] = (part + rrecv[p, d, i - 1].astype(F32)).astype(BF16)
            ring_copy(p, d, i).start()

    lane16 = lax.broadcasted_iota(jnp.int32, (16, 128), 1)
    low = lane16 < 64
    eye = (
        lax.broadcasted_iota(jnp.int32, (112, 112), 0) == lax.broadcasted_iota(jnp.int32, (112, 112), 1)
    ).astype(F32).astype(BF16)

    def finish(p):
        u, v = piece_uv(p)
        slot = p % SLOTS
        for d in range(2):
            ring_copy(p, d, 2).wait_recv()
            hidden = own[slot, zh, :, d * 128 : (d + 1) * 128] + rrecv[p, d, 2].astype(F32)
            pair = pair_at(d, u, v)
            e0 = (pair // 4) * 8 + pair % 4
            e1 = e0 + 4
            rows = jnp.concatenate(
                [gate[pl.ds(pl.multiple_of(e * 128 + d * 64, 64), 64), :] for e in (e0, e1)], axis=0
            )
            gate_t = lax.dot_general(eye, rows, NT, preferred_element_type=F32)
            up = (hidden * gate_t).astype(BF16)
            ft = lax.dot_general(auj[...], up, NN, preferred_element_type=F32)
            turned = pltpu.roll(ft, 64, 1)
            p0, p1 = proj[e0].astype(F32), proj[e1].astype(F32)
            zero = jnp.zeros_like(p0)
            if d == 0:
                fac[e0, 0:16] += jnp.where(low, ft, 0.0)
                fac[e1, 0:16] += jnp.where(low, turned, 0.0)
                q0 = jnp.where(low, p0, zero)
                q1 = jnp.where(low, zero, pltpu.roll(p1, 64, 1))
            else:
                fac[e0, 0:16] += jnp.where(low, 0.0, turned)
                fac[e1, 0:16] += jnp.where(low, 0.0, ft)
                q0 = jnp.where(low, pltpu.roll(p0, 64, 1), zero)
                q1 = jnp.where(low, zero, p1)
            both = jnp.concatenate([q0, q1], axis=0).astype(BF16)
            grad = lax.dot_general(both, up, NT, preferred_element_type=F32)
            r0 = pl.ds(pl.multiple_of(e0 * 16, 16), 16)
            r1 = pl.ds(pl.multiple_of(e1 * 16, 16), 16)
            gb[r0, :] += grad[0:16]
            gb[r1, :] += grad[16:32]

    def og_due(s):
        return jnp.minimum(1 + (4 * s + 2) // 3, 16)

    def qd_due(s):
        return jnp.clip((s - 11) * 2, 0, 16)

    gather_step(*og, 0)

    def iteration(s, _):
        @pl.when((s >= 2) & (s - 2 < PIECES))
        def _():
            ring_add(s - 2, 1)

        @pl.when((s >= 3) & (s - 3 < PIECES))
        def _():
            ring_add(s - 3, 2)

        @pl.when((s >= 1) & (s - 1 < PIECES))
        def _():
            core_add(s - 1)

        @pl.when(s < PIECES)
        def _():
            multiply(s)

        def og_step(n, _):
            gather_step(*og, n)
            return 0

        lax.fori_loop(og_due(s), og_due(s + 1), og_step, 0)

        @pl.when(s == 11)
        def _():
            loads[9].wait()
            loads[10].wait()
            gather_start(*qd)

        def qd_step(n, _):
            gather_step(*qd, n)
            return 0

        lax.fori_loop(qd_due(s), qd_due(s + 1), qd_step, 0)

        @pl.when(s == STAGES)
        def _():
            def proj_wait(o, _):
                proj_copy(o, None).wait_recv()
                return 0

            lax.fori_loop(1, 32, proj_wait, 0)

        @pl.when(s >= STAGES)
        def _():
            finish(s - STAGES)

        return 0

    loads[11].wait()
    qf[...] = qu[...].astype(F32).reshape(2048, 112)
    for r in range(16):
        qt[r] = qf[pl.ds(r, 128, stride=16), :].astype(BF16)

    lax.fori_loop(0, PIECES + STAGES, iteration, 0)

    score_b = jnp.zeros((32, 128), F32)
    for r in range(16):
        part = gb[pl.ds(r, 32, stride=16), :].astype(BF16)
        score_b += lax.dot_general(part, qt[r], NT, preferred_element_type=F32)
    fac[:, 16:24, :] = jnp.broadcast_to(score_b[:, None, :], (32, 8, 128))

    def t1_copy(o):
        return pltpu.make_async_remote_copy(
            src_ref=fac.at[(dp + o) % 32], dst_ref=t1.at[o], send_sem=t1_ss.at[o], recv_sem=t1_rs.at[o],
            device_id={"dp": (dp + o) % 32}, device_id_type=MESH,
        )

    def t1_send(o, _):
        t1_copy(o).start()
        return 0

    lax.fori_loop(1, 32, t1_send, 0)

    xd = xs[:, pl.ds(pl.multiple_of(tn * width, 128), width)]

    def meet(i, _):
        k, a = i // 4, i % 4
        rows = qbuf[k, pl.ds(a * 4, 4)].reshape(256, width)
        part = lax.dot_general(rows, xd, NT, preferred_element_type=F32).reshape(4, 2, 32, 128)
        for b in range(4):
            for half in range(2):
                start = ((a * 2 + half) * 4 + b) * 64 + k * 32
                mt[pl.ds(pl.multiple_of(start, 32), 32), :] = part[b, half]
        return 0

    lax.fori_loop(0, 8, meet, 0)
    gather_drain(*og)
    gather_drain(*qd)

    def drain(p, _):
        core_copy(p).wait_send()
        for d in range(2):
            for i in range(3):
                ring_copy(p, d, i).wait_send()
        return 0

    lax.fori_loop(0, PIECES, drain, 0)

    def proj_drain(o, _):
        proj_copy(o, None).wait_send()
        return 0

    lax.fori_loop(1, 32, proj_drain, 0)

    def t1_take(o, total):
        t1_copy(o).wait_recv()
        return total + t1[o]

    total = lax.fori_loop(1, 32, t1_take, fac[dp])

    def t2_copy(o):
        return pltpu.make_async_remote_copy(
            src_ref=t2s, dst_ref=t2.at[o], send_sem=t2_ss.at[o], recv_sem=t2_rs.at[o],
            device_id={"tensor": (tn + o) % 8}, device_id_type=MESH,
        )

    def t3_copy(o):
        return pltpu.make_async_remote_copy(
            src_ref=t3s, dst_ref=t3.at[o], send_sem=t3_ss.at[o], recv_sem=t3_rs.at[o],
            device_id={"tensor": (tn + o) % 8}, device_id_type=MESH,
        )

    t2s[...] = total[0:16]
    for o in range(1, 8):
        t2_copy(o).start()

    def t1_drain(o, _):
        t1_copy(o).wait_send()
        return 0

    lax.fori_loop(1, 32, t1_drain, 0)
    factors = total[0:16]
    for o in range(1, 8):
        t2_copy(o).wait_recv()
        factors += t2[o]

    def weigh(i, _):
        rows = mt[pl.ds(pl.multiple_of(i * 128, 128), 128), :].reshape(8, 16, 128)
        acc[pl.ds(pl.multiple_of(i * 8, 8), 8), :] = jnp.sum(rows * factors[None], axis=1)
        return 0

    lax.fori_loop(0, 16, weigh, 0)
    score_a = lax.dot_general(
        jnp.ones((8, 128), F32), acc[...], NT, precision=lax.Precision.HIGHEST, preferred_element_type=F32
    )
    t3s[...] = total[16:24] + score_a
    for o in range(1, 8):
        t3_copy(o).start()
    for o in range(1, 8):
        t2_copy(o).wait_send()
    scores = t3s[...]
    for o in range(1, 8):
        t3_copy(o).wait_recv()
        scores += t3[o]
    out = jnp.zeros((1, 16), F32)
    for j in range(8):
        out = jnp.where(tn == j, scores[0:1, j * 16 : (j + 1) * 16], out)
    out_ref[...] = out
    for o in range(1, 8):
        t3_copy(o).wait_send()


def shards(x, og, gate, codes, bsc, osc, ad, au, qd, qu):
    qd = qd.reshape(64, 1024)
    dma = pltpu.SemaphoreType.DMA
    vmem = pltpu.VMEM
    return pl.pallas_call(
        kernel,
        out_shape=jax.ShapeDtypeStruct((1, 16), F32),
        in_specs=[ANY] * 10,
        out_specs=pl.BlockSpec(memory_space=pltpu.VMEM),
        scratch_shapes=[
            vmem((2, 16, 2, 64, 1024), BF16),
            vmem((2, 16, 2, 32, 1024), BF16),
            vmem((896, 1024), jnp.int32),
            vmem((14, 1024), jnp.int32),
            vmem((14, 16), F32),
            vmem((14, 1024), F32),
            vmem((896, 1024), BF16),
            vmem((128, 8192), BF16),
            vmem((16, 8192), BF16),
            vmem((16, 896), BF16),
            vmem((16, 112), BF16),
            vmem((4096, 112), BF16),
            vmem((128, 16, 112), BF16),
            vmem((2048, 112), F32),
            vmem((16, 128, 112), BF16),
            vmem((8, 112, 256), F32),
            vmem((SLOTS, 4, 112, 256), F32),
            vmem((PIECES, 4, 112, 256), BF16),
            vmem((PIECES, 4, 112, 256), BF16),
            vmem((PIECES, 2, 3, 112, 128), BF16),
            vmem((PIECES, 2, 3, 112, 128), BF16),
            vmem((32, 16, 128), BF16),
            vmem((512, 112), F32),
            vmem((32, 24, 128), F32),
            vmem((32, 24, 128), F32),
            vmem((16, 128), F32),
            vmem((8, 16, 128), F32),
            vmem((2048, 128), F32),
            vmem((128, 128), F32),
            vmem((8, 128), F32),
            vmem((8, 8, 128), F32),
            dma((12,)),
            dma((2, 4, 4, 2)),
            dma((2, 4, 4, 2)),
            dma((2, 4, 4, 2)),
            dma((2, 4, 4, 2)),
            dma((PIECES,)),
            dma((PIECES,)),
            dma((PIECES, 2, 3)),
            dma((PIECES, 2, 3)),
            dma((32,)),
            dma((32,)),
            dma((32,)),
            dma((32,)),
            dma((8,)),
            dma((8,)),
            dma((8,)),
            dma((8,)),
        ],
        compiler_params=pltpu.CompilerParams(
            collective_id=0, has_side_effects=True, vmem_limit_bytes=60 * 1024 * 1024
        ),
        name="influence",
    )(x, og, gate, codes, bsc, osc, ad, au, qd, qu)


def solution(mesh):
    in_specs = (
        P("dp", None),
        P("dp", "tensor"),
        P(None, ("dp", "tensor")),
        P("dp", "tensor"),
        P("dp", "tensor"),
        P("dp", "tensor"),
        P(),
        P(None, "dp"),
        P("dp", None, "tensor"),
        P(None, None, ("dp", "tensor")),
    )
    return jax.shard_map(shards, mesh=mesh, in_specs=in_specs, out_specs=P("dp", "tensor"), check_vma=False)
```

```python
import jax
import jax.numpy as jnp
from jax import lax
from jax.experimental import pallas as pl
from jax.experimental.pallas import tpu as pltpu
from jax.sharding import PartitionSpec as P

MESH = pl.DeviceIdType.MESH
F32 = jnp.float32
BF16 = jnp.bfloat16
NT = (((1,), (1,)), ((), ()))
NN = (((1,), (0,)), ((), ()))
ANY = pl.BlockSpec(memory_space=pl.ANY)

PIECES = 16
SLOTS = 8
LAG = 2
STAGES = 1 + 3 * LAG

LEVELS = (
    -1.0,
    -0.6961928009986877,
    -0.5250730514526367,
    -0.39491748809814453,
    -0.28444138169288635,
    -0.18477343022823334,
    -0.09105003625154495,
    0.0,
    0.07958029955625534,
    0.16093020141124725,
    0.24611230194568634,
    0.33791524171829224,
    0.44070982933044434,
    0.5626170039176941,
    0.7229568362236023,
    1.0,
)


def lookup(codes):
    values = [jnp.full(codes.shape, level, F32) for level in LEVELS]
    for bit in range(4):
        odd = (codes & (1 << bit)) != 0
        values = [jnp.where(odd, values[i + 1], values[i]) for i in range(0, len(values), 2)]
    return values[0]


def offset(k):
    return k + k // 2 - 2 * (k // 3)


ORDER = (
    (0, 0), (1, 0), (2, 0), (0, 1), (0, 2), (3, 0), (0, 3), (1, 1),
    (1, 2), (2, 1), (2, 2), (1, 3), (3, 1), (3, 2), (2, 3), (3, 3),
)


def piece_uv(n):
    u = v = 0
    for i, (a, b) in enumerate(ORDER):
        u = jnp.where(n == i, a, u)
        v = jnp.where(n == i, b, v)
    return u, v


OG_BEFORE = {1: [("take", 1, 0)]}
OG_AFTER = {
    1: [("take", 2, 0), ("take", 0, 1), ("take", 0, 2), ("second", 1)],
    2: [("second", 2)],
    3: [("take", 3, 0)],
    4: [("second", 3), ("take", 0, 3)],
    5: [("take", 1, 1), ("take", 1, 2)],
    7: [("take", 2, 1), ("take", 2, 2)],
    8: [("take", 1, 3)],
    9: [("take", 3, 1), ("take", 3, 2)],
    10: [("take", 2, 3)],
    12: [("take", 3, 3)],
}
QD_AFTER = {
    8: [("start",)],
    9: [("take", 0, 0)],
    11: [("take", 1, 0), ("take", 2, 0), ("take", 0, 1), ("take", 0, 2), ("second", 1)],
    12: [("second", 2)],
    13: [("take", 3, 0), ("second", 3), ("take", 0, 3)],
    14: [("take", 1, 1), ("take", 1, 2)],
    16: [("take", 2, 1), ("take", 2, 2)],
    18: [("take", 3, 1), ("take", 3, 2)],
    19: [("take", 1, 3), ("take", 2, 3)],
    21: [("take", 3, 3)],
}


def kernel(
    x_hbm, og_hbm, gate_hbm, codes_hbm, bsc_hbm, osc_hbm, ad_hbm, au_hbm, qd_hbm, qu_hbm,
    out_ref,
    buf, qbuf, codes, bsc, osc, scale, w, xs, ad, au, auj, gate, qu,
    prod, own, csend, crecv, rsend, rrecv, proj, gb, fac, t1, t2s, t2, sbs, t1b, mt, acc, t3s, t3,
    lsem, og_ss, og_rs, qd_ss, qd_rs, c_ss, c_rs, r_ss, r_rs, p_ss, p_rs, t1_ss, t1_rs, t1b_ss, t1b_rs, t2_ss, t2_rs, t3_ss, t3_rs,
):
    dp = lax.axis_index("dp")
    tn = lax.axis_index("tensor")
    y, l, x = dp % 4, (dp // 4) % 2, dp // 8
    zh, c = tn // 2, tn % 2

    width = og_hbm.shape[1]
    here = x * 4 + y
    loads = [
        (og_hbm.at[pl.ds(0, 64)], buf.at[0, here, l]),
        (og_hbm.at[pl.ds(64, 64)], buf.at[1, here, l]),
        (codes_hbm, codes),
        (bsc_hbm, bsc),
        (osc_hbm, osc),
        (x_hbm, xs),
        (ad_hbm, ad),
        (au_hbm, au),
        (gate_hbm, gate),
        (qd_hbm.at[pl.ds(0, 32)], qbuf.at[0, here, l]),
        (qd_hbm.at[pl.ds(32, 32)], qbuf.at[1, here, l]),
        (qu_hbm, qu),
    ]
    loads = [pltpu.make_async_copy(a, b, lsem.at[i]) for i, (a, b) in enumerate(loads)]
    for load in loads:
        load.start()

    barrier = pltpu.get_barrier_semaphore()

    def greet_dp(o, _):
        pl.semaphore_signal(barrier, 1, device_id={"dp": (dp + o) % 32}, device_id_type=MESH)
        return 0

    def greet_tn(o, _):
        pl.semaphore_signal(barrier, 1, device_id={"tensor": (tn + o) % 8}, device_id_type=MESH)
        return 0

    lax.fori_loop(1, 32, greet_dp, 0)
    lax.fori_loop(1, 8, greet_tn, 0)
    pl.semaphore_wait(barrier, 38)

    def pair_at(k, u, v):
        a, b = offset(u), offset(v)
        if k == 0:
            return ((x + a) % 4) * 4 + (y + b) % 4
        return ((x + b) % 4) * 4 + (y + a) % 4

    def near(k, first, step):
        along_x = first == (k == 0)
        if along_x:
            return {"dp": (((x + step) % 4) * 2 + l) * 4 + y}
        return {"dp": (x * 2 + l) * 4 + (y + step) % 4}

    def piece_copy(data, ss, rs, k, u, v, half, ur, vr, target):
        ref = data.at[k, pair_at(k, u, v)]
        sem = 0 if half is None else half
        ref = ref if half is None else ref.at[half]
        return pltpu.make_async_remote_copy(
            src_ref=ref, dst_ref=ref, send_sem=ss.at[k, ur, vr, sem], recv_sem=rs.at[k, ur, vr, sem],
            device_id=target, device_id_type=MESH,
        )

    partner = {"dp": (x * 2 + 1 - l) * 4 + y}

    def halves(u, v):
        return (0, 1) if u == 0 or v == 0 or v == 3 else (None,)

    def gather_own(data, ss, rs, k, half):
        piece_copy(data, ss, rs, k, 0, 0, half, 2, 0, near(k, True, 1)).start()
        piece_copy(data, ss, rs, k, 0, 0, half, 1, 0, near(k, True, 3)).start()
        piece_copy(data, ss, rs, k, 0, 0, half, 0, 2, near(k, False, 1)).start()
        piece_copy(data, ss, rs, k, 0, 0, half, 0, 1, near(k, False, 3)).start()

    def gather_start(data, ss, rs):
        for k in range(2):
            piece_copy(data, ss, rs, k, 0, 0, l, 0, 0, partner).start()
        for k in range(2):
            gather_own(data, ss, rs, k, l)

    def gather_second(data, ss, rs, u):
        for k in range(2):
            piece_copy(data, ss, rs, k, u, 0, None, u, 2, near(k, False, 1)).start()
            piece_copy(data, ss, rs, k, u, 0, None, u, 1, near(k, False, 3)).start()

    def gather_take(data, ss, rs, u, v):
        for k in range(2):
            if (u, v) == (0, 0):
                piece_copy(data, ss, rs, k, 0, 0, 1 - l, 0, 0, partner).wait_recv()
                gather_own(data, ss, rs, k, 1 - l)
                continue
            for half in halves(u, v):
                piece_copy(data, ss, rs, k, u, v, half, u, v, partner).wait_recv()
            if v == 0 and u < 3:
                half = 2 - u
                piece_copy(data, ss, rs, k, u, 0, half, 3, 0, near(k, True, 3 if u == 1 else 1)).start()
            if v in (1, 2):
                half = 2 - v
                piece_copy(data, ss, rs, k, u, v, half, u, 3, near(k, False, 3 if v == 1 else 1)).start()

    def gather_do(gather, actions):
        for action in actions:
            {"start": gather_start, "second": gather_second, "take": gather_take}[action[0]](*gather, *action[1:])

    def gather_drain(data, ss, rs):
        for k in range(2):
            for u in range(4):
                for v in range(4):
                    for half in ((l,) if u == v == 0 else halves(u, v)):
                        piece_copy(data, ss, rs, k, 0, 0, half, u, v, partner).wait_send()

    og = (buf, og_ss, og_rs)
    qd = (qbuf, qd_ss, qd_rs)

    loads[0].wait()
    loads[1].wait()
    gather_start(*og)

    def proj_copy(o, to):
        return pltpu.make_async_remote_copy(
            src_ref=proj.at[dp], dst_ref=proj.at[dp], send_sem=p_ss.at[o], recv_sem=p_rs.at[o],
            device_id={"dp": (dp + o) % 32}, device_id_type=MESH,
        )

    def proj_send(o, _):
        proj_copy(o, None).start()
        return 0

    loads[3].wait()
    loads[4].wait()
    lane14 = lax.broadcasted_iota(jnp.int32, (14, 128), 1)
    for col in range(width // 128):
        pick = jnp.where(
            lane14 < 64,
            jnp.broadcast_to(osc[:, 2 * col : 2 * col + 1], (14, 128)),
            jnp.broadcast_to(osc[:, 2 * col + 1 : 2 * col + 2], (14, 128)),
        )
        at = pl.ds(col * 128, 128)
        scale[:, at] = (bsc[:, at] + 1).astype(F32) / 256.0 * pick
    loads[2].wait()

    def dequant(b, _):
        rows = pl.ds(pl.multiple_of(b * 64, 64), 64)
        w[rows, :] = (lookup(codes[rows, :]) * scale[pl.ds(b, 1), :]).astype(BF16)
        return 0

    lax.fori_loop(0, 14, dequant, 0)

    loads[7].wait()
    mine = jnp.zeros((16, 112), F32)
    for j in range(8):
        mine = jnp.where(tn == j, au[:, j * 112 : (j + 1) * 112].astype(F32), mine)
    auj[...] = mine.astype(BF16)
    gb[...] = jnp.zeros_like(gb)
    fac[...] = jnp.zeros_like(fac)
    loads[8].wait()

    def core_copy(p):
        return pltpu.make_async_remote_copy(
            src_ref=csend.at[p], dst_ref=crecv.at[p], send_sem=c_ss.at[p], recv_sem=c_rs.at[p],
            device_id={"tensor": zh * 2 + 1 - c}, device_id_type=MESH,
        )

    def ring_copy(p, d, i):
        step = 1 if d == 0 else 3
        return pltpu.make_async_remote_copy(
            src_ref=rsend.at[p, d, i], dst_ref=rrecv.at[p, d, i], send_sem=r_ss.at[p, d, i],
            recv_sem=r_rs.at[p, d, i],
            device_id={"tensor": ((zh + step) % 4) * 2 + c}, device_id_type=MESH,
        )

    def ring_target(d, i):
        return (zh + (3 - i if d == 0 else i + 1)) % 4

    def multiply(p):
        u, v = piece_uv(p)
        rows = jnp.concatenate(
            [buf[0, pair_at(0, u, v)].reshape(128, width), buf[1, pair_at(1, u, v)].reshape(128, width)], axis=0
        )
        prod[...] = lax.dot_general(w[...], rows, NT, preferred_element_type=F32).reshape(8, 112, 256)
        slot = p % SLOTS
        for k in range(4):
            csend[p, k] = prod[2 * k + 1 - c].astype(BF16)
            own[slot, k] = prod[2 * k + c]
        core_copy(p).start()

    def core_add(p):
        core_copy(p).wait_recv()
        slot = p % SLOTS
        for k in range(4):
            own[slot, k] += crecv[p, k].astype(F32)
        for d in range(2):
            rsend[p, d, 0] = own[slot, ring_target(d, 0), :, d * 128 : (d + 1) * 128].astype(BF16)
            ring_copy(p, d, 0).start()

    def ring_add(p, i):
        slot = p % SLOTS
        for d in range(2):
            ring_copy(p, d, i - 1).wait_recv()
            part = own[slot, ring_target(d, i), :, d * 128 : (d + 1) * 128]
            rsend[p, d, i] = (part + rrecv[p, d, i - 1].astype(F32)).astype(BF16)
            ring_copy(p, d, i).start()

    lane16 = lax.broadcasted_iota(jnp.int32, (16, 128), 1)
    low = lane16 < 64
    low112 = lax.broadcasted_iota(jnp.int32, (112, 128), 1) < 64

    def finish(p):
        u, v = piece_uv(p)
        slot = p % SLOTS
        for d in range(2):
            ring_copy(p, d, 2).wait_recv()
            hidden = own[slot, zh, :, d * 128 : (d + 1) * 128] + rrecv[p, d, 2].astype(F32)
            pair = pair_at(d, u, v)
            e0 = (pair // 4) * 8 + pair % 4
            e1 = e0 + 4
            g0, g1 = [gate[:, pl.ds(pl.multiple_of(e * 128, 128), 128)].astype(F32) for e in (e0, e1)]
            if d == 0:
                g1 = pltpu.roll(g1, 64, 1)
            else:
                g0 = pltpu.roll(g0, 64, 1)
            up = (hidden * jnp.where(low112, g0, g1)).astype(BF16)
            ft = lax.dot_general(auj[...], up, NN, preferred_element_type=F32)
            turned = pltpu.roll(ft, 64, 1)
            p0, p1 = proj[e0].astype(F32), proj[e1].astype(F32)
            zero = jnp.zeros_like(p0)
            if d == 0:
                fac[e0] += jnp.where(low, ft, 0.0)
                fac[e1] += jnp.where(low, turned, 0.0)
                q0 = jnp.where(low, p0, zero)
                q1 = jnp.where(low, zero, pltpu.roll(p1, 64, 1))
            else:
                fac[e0] += jnp.where(low, 0.0, turned)
                fac[e1] += jnp.where(low, 0.0, ft)
                q0 = jnp.where(low, pltpu.roll(p0, 64, 1), zero)
                q1 = jnp.where(low, zero, p1)
            both = jnp.concatenate([q0, q1], axis=0).astype(BF16)
            grad = lax.dot_general(both, up, NT, preferred_element_type=F32)
            r0 = pl.ds(pl.multiple_of(e0 * 16, 16), 16)
            r1 = pl.ds(pl.multiple_of(e1 * 16, 16), 16)
            gb[r0, :] += grad[0:16]
            gb[r1, :] += grad[16:32]

    def t1_copy(o):
        return pltpu.make_async_remote_copy(
            src_ref=fac.at[(dp + o) % 32], dst_ref=t1.at[o], send_sem=t1_ss.at[o], recv_sem=t1_rs.at[o],
            device_id={"dp": (dp + o) % 32}, device_id_type=MESH,
        )

    def t1b_copy(o):
        return pltpu.make_async_remote_copy(
            src_ref=sbs.at[(dp + o) % 32], dst_ref=t1b.at[o], send_sem=t1b_ss.at[o], recv_sem=t1b_rs.at[o],
            device_id={"dp": (dp + o) % 32}, device_id_type=MESH,
        )

    def hand_over(p):
        for i, (u, v) in enumerate(ORDER):
            if ORDER.index((v, u)) > i:
                continue

            @pl.when(p == i)
            def _(u=u, v=v):
                for a, b in {(u, v), (v, u)} if u != v else {(u, u)}:
                    pair = pair_at(0, a, b)
                    for half in range(2):
                        e = (pair // 4 * 2 + half) * 4 + pair % 4
                        if a == b == 0:

                            @pl.when(half != l)
                            def _(e=e):
                                t1_copy((e + 32 - dp) % 32).start()
                        else:
                            t1_copy((e + 32 - dp) % 32).start()

    loads[5].wait()
    loads[6].wait()
    proj[dp] = lax.dot_general(ad[...], xs[...], NT, preferred_element_type=F32).astype(BF16)
    gather_take(*og, 0, 0)

    def iteration(s, _):
        @pl.when((s >= 1 + LAG) & (s - 1 - LAG < PIECES))
        def _():
            ring_add(s - 1 - LAG, 1)

        @pl.when((s >= 1 + 2 * LAG) & (s - 1 - 2 * LAG < PIECES))
        def _():
            ring_add(s - 1 - 2 * LAG, 2)

        @pl.when((s >= 1) & (s - 1 < PIECES))
        def _():
            core_add(s - 1)

        for at, actions in OG_BEFORE.items():

            @pl.when(s == at)
            def _(actions=actions):
                gather_do(og, actions)

        @pl.when(s < PIECES)
        def _():
            multiply(s)

        @pl.when(s < 4)
        def _():
            lax.fori_loop(jnp.maximum(8 * s, 1), 8 * s + 8, proj_send, 0)

        for at, actions in OG_AFTER.items():

            @pl.when(s == at)
            def _(actions=actions):
                gather_do(og, actions)

        for at, actions in QD_AFTER.items():

            @pl.when(s == at)
            def _(actions=actions):
                if actions[0][0] == "start":
                    loads[9].wait()
                    loads[10].wait()
                gather_do(qd, actions)

        @pl.when(s == STAGES)
        def _():
            def proj_wait(o, _):
                proj_copy(o, None).wait_recv()
                return 0

            lax.fori_loop(1, 32, proj_wait, 0)

        @pl.when(s >= STAGES)
        def _():
            finish(s - STAGES)
            hand_over(s - STAGES)

        return 0

    loads[11].wait()
    lax.fori_loop(0, PIECES + STAGES, iteration, 0)

    def t1_take(o, total):
        t1_copy(o).wait_recv()
        return total + t1[o]

    def t2_copy(o):
        return pltpu.make_async_remote_copy(
            src_ref=t2s, dst_ref=t2.at[o], send_sem=t2_ss.at[o], recv_sem=t2_rs.at[o],
            device_id={"tensor": (tn + o) % 8}, device_id_type=MESH,
        )

    t2s[...] = lax.fori_loop(1, 32, t1_take, fac[dp])
    for o in range(1, 8):
        t2_copy(o).start()

    score_b = jnp.zeros((32, 128), F32)
    for r in range(16):
        part = gb[pl.ds(r, 32, stride=16), :].astype(BF16)
        score_b += lax.dot_general(part, qu[r], NN, preferred_element_type=F32)
    sbs[...] = jnp.broadcast_to(score_b[:, None, :], (32, 8, 128))

    def t1b_send(o, _):
        t1b_copy(o).start()
        return 0

    lax.fori_loop(1, 32, t1b_send, 0)

    xd = xs[:, pl.ds(pl.multiple_of(tn * width, 128), width)]

    def meet(i, _):
        k, a = i // 4, i % 4
        rows = qbuf[k, pl.ds(a * 4, 4)].reshape(256, width)
        part = lax.dot_general(rows, xd, NT, preferred_element_type=F32).reshape(4, 2, 32, 128)
        for b in range(4):
            for half in range(2):
                start = ((a * 2 + half) * 4 + b) * 64 + k * 32
                mt[pl.ds(pl.multiple_of(start, 32), 32), :] = part[b, half]
        return 0

    lax.fori_loop(0, 8, meet, 0)
    factors = t2s[...]
    for o in range(1, 8):
        t2_copy(o).wait_recv()
        factors += t2[o]

    def t3_copy(o):
        return pltpu.make_async_remote_copy(
            src_ref=t3s, dst_ref=t3.at[o], send_sem=t3_ss.at[o], recv_sem=t3_rs.at[o],
            device_id={"tensor": (tn + o) % 8}, device_id_type=MESH,
        )

    def weigh(i, _):
        rows = mt[pl.ds(pl.multiple_of(i * 128, 128), 128), :].reshape(8, 16, 128)
        acc[pl.ds(pl.multiple_of(i * 8, 8), 8), :] = jnp.sum(rows * factors[None], axis=1)
        return 0

    lax.fori_loop(0, 16, weigh, 0)
    score_a = lax.dot_general(
        jnp.ones((8, 128), F32), acc[...], NT, precision=lax.Precision.HIGHEST, preferred_element_type=F32
    )

    def t1b_take(o, total):
        t1b_copy(o).wait_recv()
        return total + t1b[o]

    t3s[...] = lax.fori_loop(1, 32, t1b_take, sbs[dp] + score_a)
    for o in range(1, 8):
        t3_copy(o).start()
    gather_drain(*og)
    gather_drain(*qd)

    def drain(p, _):
        core_copy(p).wait_send()
        for d in range(2):
            for i in range(3):
                ring_copy(p, d, i).wait_send()
        return 0

    lax.fori_loop(0, PIECES, drain, 0)

    def proj_drain(o, _):
        proj_copy(o, None).wait_send()
        return 0

    lax.fori_loop(1, 32, proj_drain, 0)

    def t1_drain(o, _):
        t1_copy(o).wait_send()
        t1b_copy(o).wait_send()
        return 0

    lax.fori_loop(1, 32, t1_drain, 0)
    for o in range(1, 8):
        t2_copy(o).wait_send()
    scores = t3s[...]
    for o in range(1, 8):
        t3_copy(o).wait_recv()
        scores += t3[o]
    out = jnp.zeros((1, 16), F32)
    for j in range(8):
        out = jnp.where(tn == j, scores[0:1, j * 16 : (j + 1) * 16], out)
    out_ref[...] = out
    for o in range(1, 8):
        t3_copy(o).wait_send()


def shards(x, og, gate, codes, bsc, osc, ad, au, qd, qu):
    qd = qd.reshape(64, 1024)
    gate = gate.T
    qu = qu.transpose(1, 2, 0)
    dma = pltpu.SemaphoreType.DMA
    vmem = pltpu.VMEM
    return pl.pallas_call(
        kernel,
        out_shape=jax.ShapeDtypeStruct((1, 16), F32),
        in_specs=[ANY] * 10,
        out_specs=pl.BlockSpec(memory_space=pltpu.VMEM),
        scratch_shapes=[
            vmem((2, 16, 2, 64, 1024), BF16),
            vmem((2, 16, 2, 32, 1024), BF16),
            vmem((896, 1024), jnp.int32),
            vmem((14, 1024), jnp.int32),
            vmem((14, 16), F32),
            vmem((14, 1024), F32),
            vmem((896, 1024), BF16),
            vmem((128, 8192), BF16),
            vmem((16, 8192), BF16),
            vmem((16, 896), BF16),
            vmem((16, 112), BF16),
            vmem((112, 4096), BF16),
            vmem((16, 112, 128), BF16),
            vmem((8, 112, 256), F32),
            vmem((SLOTS, 4, 112, 256), F32),
            vmem((PIECES, 4, 112, 256), BF16),
            vmem((PIECES, 4, 112, 256), BF16),
            vmem((PIECES, 2, 3, 112, 128), BF16),
            vmem((PIECES, 2, 3, 112, 128), BF16),
            vmem((32, 16, 128), BF16),
            vmem((512, 112), F32),
            vmem((32, 16, 128), F32),
            vmem((32, 16, 128), F32),
            vmem((16, 128), F32),
            vmem((8, 16, 128), F32),
            vmem((32, 8, 128), F32),
            vmem((32, 8, 128), F32),
            vmem((2048, 128), F32),
            vmem((128, 128), F32),
            vmem((8, 128), F32),
            vmem((8, 8, 128), F32),
            dma((12,)),
            dma((2, 4, 4, 2)),
            dma((2, 4, 4, 2)),
            dma((2, 4, 4, 2)),
            dma((2, 4, 4, 2)),
            dma((PIECES,)),
            dma((PIECES,)),
            dma((PIECES, 2, 3)),
            dma((PIECES, 2, 3)),
            dma((32,)),
            dma((32,)),
            dma((32,)),
            dma((32,)),
            dma((32,)),
            dma((32,)),
            dma((8,)),
            dma((8,)),
            dma((8,)),
            dma((8,)),
        ],
        compiler_params=pltpu.CompilerParams(
            collective_id=0, has_side_effects=True, vmem_limit_bytes=60 * 1024 * 1024
        ),
        name="influence",
    )(x, og, gate, codes, bsc, osc, ad, au, qd, qu)


def solution(mesh):
    in_specs = (
        P("dp", None),
        P("dp", "tensor"),
        P(None, ("dp", "tensor")),
        P("dp", "tensor"),
        P("dp", "tensor"),
        P("dp", "tensor"),
        P(),
        P(None, "dp"),
        P("dp", None, "tensor"),
        P(None, None, ("dp", "tensor")),
    )
    return jax.shard_map(shards, mesh=mesh, in_specs=in_specs, out_specs=P("dp", "tensor"), check_vma=False)
```

```python
import jax
import jax.numpy as jnp
from jax import lax
from jax.experimental import pallas as pl
from jax.experimental.pallas import tpu as pltpu
from jax.sharding import PartitionSpec as P

MESH = pl.DeviceIdType.MESH
F32 = jnp.float32
BF16 = jnp.bfloat16
NT = (((1,), (1,)), ((), ()))
NN = (((1,), (0,)), ((), ()))
ANY = pl.BlockSpec(memory_space=pl.ANY)

PIECES = 16
SLOTS = 8
LAG = 2
STAGES = 1 + 3 * LAG

LEVELS = (
    -1.0,
    -0.6961928009986877,
    -0.5250730514526367,
    -0.39491748809814453,
    -0.28444138169288635,
    -0.18477343022823334,
    -0.09105003625154495,
    0.0,
    0.07958029955625534,
    0.16093020141124725,
    0.24611230194568634,
    0.33791524171829224,
    0.44070982933044434,
    0.5626170039176941,
    0.7229568362236023,
    1.0,
)


def lookup(codes):
    values = [jnp.full(codes.shape, level, F32) for level in LEVELS]
    for bit in range(4):
        odd = (codes & (1 << bit)) != 0
        values = [jnp.where(odd, values[i + 1], values[i]) for i in range(0, len(values), 2)]
    return values[0]


def offset(k):
    return k + k // 2 - 2 * (k // 3)


OWN, OTHER = 2, 3
WHOLE = [(0, 0), (3, 0), (0, 3), (1, 1), (1, 2), (2, 1), (2, 2), (1, 3), (3, 1), (3, 2), (2, 3), (3, 3)]
WHOLE = [((u, v, 0), (u, v, 1)) for u, v in WHOLE]
ORDER = [
    ((1, 0, OWN), (2, 0, OWN)),
    WHOLE[0],
    ((0, 1, OWN), (0, 2, OWN)),
    ((1, 0, OTHER), (2, 0, OTHER)),
    ((0, 1, OTHER), (0, 2, OTHER)),
] + WHOLE[1:]
PLACE = {part: i for i, parts in enumerate(ORDER) for part in parts}


def complete_at(p):
    return [(u, v, w) for (u, v, w), i in PLACE.items() if max(i, PLACE[v, u, w]) == p]


def piece_parts(n):
    found = []
    for side in range(2):
        code = pick(n, {i: offset(u) + 4 * offset(v) + 16 * w for i, (u, v, w) in enumerate(parts[side] for parts in ORDER)})
        found.append((code & 3, (code >> 2) & 3, code >> 4))
    return found


def pick(n, table):
    value = 0
    for i, entry in table.items():
        value = jnp.where(n == i, entry, value)
    return value


def takes(*places):
    return [("take", u, v, w) for u, v in places for w in (OWN, OTHER)]


OG_BEFORE = {
    0: [("take", 1, 0, OWN), ("take", 2, 0, OWN)],
    1: [("take", 0, 0, OTHER)],
    3: [("take", 1, 0, OTHER), ("take", 2, 0, OTHER)],
}
OG_AFTER = {
    1: [("take", 0, 1, OWN), ("take", 0, 2, OWN)],
    3: [("take", 0, 1, OTHER), ("take", 0, 2, OTHER), ("second", 1)],
    4: takes((3, 0)) + [("second", 2)],
    5: takes((0, 3)) + [("second", 3)],
    6: [("whole", 1, 1), ("whole", 1, 2)],
    8: [("whole", 2, 1), ("whole", 2, 2)],
    9: takes((1, 3)),
    10: [("whole", 3, 1), ("whole", 3, 2)],
    11: takes((2, 3)),
    13: takes((3, 3)),
}
QD_AFTER = {
    9: [("start",), ("more",)],
    10: [("take", 0, 0, OTHER)],
    12: takes((1, 0), (2, 0), (0, 1), (0, 2)) + [("second", 1), ("second", 2)],
    13: takes((3, 0), (0, 3)) + [("second", 3)],
    14: [("whole", 1, 1), ("whole", 1, 2)],
    15: [("whole", 2, 1), ("whole", 2, 2)],
    17: [("whole", 3, 1), ("whole", 3, 2)] + takes((1, 3)),
    18: takes((2, 3)),
    19: takes((3, 3)),
}
MEET = [(0, 0), (1, 0), (2, 0), (0, 1), (0, 2), (3, 0), (0, 3), (1, 1), (1, 2), (2, 1), (2, 2), (3, 1), (3, 2), (1, 3), (2, 3), (3, 3)]
MET = {10: 1, 12: 5, 13: 7, 14: 9, 15: 11, 17: 14, 18: 15, 19: 16}
EARLY = 12


def kernel(
    x_hbm, og_hbm, gate_hbm, codes_hbm, bsc_hbm, osc_hbm, ad_hbm, au_hbm, qd_hbm, qu_hbm,
    out_ref,
    buf, qbuf, codes, bsc, osc, scale, w, xs, ad, au, auj, gate, qu,
    prod, csend, crecv, rsend, rrecv, proj, gb, fac, t1, t2s, t2, sbs, sbl, t1b, mt, acc, t3s, t3,
    lsem, og_ss, og_rs, qd_ss, qd_rs, c_ss, c_rs, r_ss, r_rs, p_ss, p_rs, t1_ss, t1_rs, t1b_ss, t1b_rs, t2_ss, t2_rs, t3_ss, t3_rs,
):
    dp = lax.axis_index("dp")
    tn = lax.axis_index("tensor")
    y, l, x = dp & 3, (dp >> 2) & 1, dp >> 3
    zh, c = tn >> 1, tn & 1

    width = og_hbm.shape[1]
    here = x * 4 + y
    loads = [
        (og_hbm.at[pl.ds(0, 64)], buf.at[0, here, l]),
        (og_hbm.at[pl.ds(64, 64)], buf.at[1, here, l]),
        (codes_hbm, codes),
        (bsc_hbm, bsc),
        (osc_hbm, osc),
        (x_hbm, xs),
        (ad_hbm, ad),
        (au_hbm, au),
        (gate_hbm, gate),
        (qd_hbm.at[pl.ds(0, 32)], qbuf.at[0, here, l]),
        (qd_hbm.at[pl.ds(32, 32)], qbuf.at[1, here, l]),
        (qu_hbm, qu),
    ]
    loads = [pltpu.make_async_copy(a, b, lsem.at[i]) for i, (a, b) in enumerate(loads)]
    for load in loads:
        load.start()

    barrier = pltpu.get_barrier_semaphore()

    def greet_dp(o, _):
        pl.semaphore_signal(barrier, 1, device_id={"dp": ((dp + o) & 31)}, device_id_type=MESH)
        return 0

    def greet_tn(o, _):
        pl.semaphore_signal(barrier, 1, device_id={"tensor": ((tn + o) & 7)}, device_id_type=MESH)
        return 0

    lax.fori_loop(1, 32, greet_dp, 0)
    lax.fori_loop(1, 8, greet_tn, 0)
    pl.semaphore_wait(barrier, 38)

    def pair_of(k, a, b):
        if k == 1:
            a, b = b, a
        return ((x + a) & 3) * 4 + ((y + b) & 3)

    def pair_at(k, u, v):
        return pair_of(k, offset(u), offset(v))

    def near(k, first, step):
        along_x = first == (k == 0)
        if along_x:
            return {"dp": (((x + step) & 3) * 2 + l) * 4 + y}
        return {"dp": (x * 2 + l) * 4 + ((y + step) & 3)}

    def piece_copy(data, ss, rs, k, u, v, half, ur, vr, target):
        ref = data.at[k, pair_at(k, u, v)]
        sem = 0 if half is None else half
        ref = ref if half is None else ref.at[half]
        return pltpu.make_async_remote_copy(
            src_ref=ref, dst_ref=ref, send_sem=ss.at[k, ur, vr, sem], recv_sem=rs.at[k, ur, vr, sem],
            device_id=target, device_id_type=MESH,
        )

    partner = {"dp": (x * 2 + 1 - l) * 4 + y}

    def half_of(w):
        if isinstance(w, int):
            return w if w < 2 else l if w == OWN else 1 - l
        return jnp.where(w < 2, w, jnp.where(w == OWN, l, 1 - l))

    def gather_first(data, ss, rs, k, half):
        piece_copy(data, ss, rs, k, 0, 0, half, 2, 0, near(k, True, 1)).start()
        piece_copy(data, ss, rs, k, 0, 0, half, 1, 0, near(k, True, 3)).start()

    def gather_more(data, ss, rs, half=None):
        half = l if half is None else half
        for k in range(2):
            piece_copy(data, ss, rs, k, 0, 0, half, 0, 2, near(k, False, 1)).start()
            piece_copy(data, ss, rs, k, 0, 0, half, 0, 1, near(k, False, 3)).start()

    def gather_start(data, ss, rs):
        for k in range(2):
            piece_copy(data, ss, rs, k, 0, 0, l, 0, 0, partner).start()
            gather_first(data, ss, rs, k, l)

    def gather_second(data, ss, rs, u):
        for k in range(2):
            piece_copy(data, ss, rs, k, u, 0, None, u, 2, near(k, False, 1)).start()
            piece_copy(data, ss, rs, k, u, 0, None, u, 1, near(k, False, 3)).start()

    def gather_take(data, ss, rs, u, v, w):
        half = half_of(w)
        for k in range(2):
            piece_copy(data, ss, rs, k, u, v, half, u, v, partner).wait_recv()
            if (u, v) == (0, 0):
                gather_first(data, ss, rs, k, half)
            if (u, v) in ((1, 0), (2, 0), (0, 1), (0, 2)):
                step, at = (3, 1) if 1 in (u, v) else (1, 0)
                ur, vr = (3, 0) if v == 0 else (0, 3)

                @pl.when(half == at)
                def _(k=k, step=step, at=at, ur=ur, vr=vr):
                    piece_copy(data, ss, rs, k, u, v, at, ur, vr, near(k, v == 0, step)).start()
        if (u, v) == (0, 0):
            gather_more(data, ss, rs, half)

    def gather_whole(data, ss, rs, u, v):
        for k in range(2):
            piece_copy(data, ss, rs, k, u, v, None, u, v, partner).wait_recv()
            step, at = (3, 1) if v == 1 else (1, 0)
            piece_copy(data, ss, rs, k, u, v, at, u, 3, near(k, False, step)).start()

    def gather_do(gather, actions):
        for action in actions:
            act = {
                "start": gather_start, "more": gather_more, "second": gather_second,
                "take": gather_take, "whole": gather_whole,
            }[action[0]]
            act(*gather, *action[1:])

    def gather_drain(data, ss, rs):
        for k in range(2):
            for u in range(4):
                for v in range(4):
                    pieces = (l,) if u == v == 0 else (0, 1) if u == 0 or v in (0, 3) else (None,)
                    for half in pieces:
                        piece_copy(data, ss, rs, k, 0, 0, half, u, v, partner).wait_send()

    og = (buf, og_ss, og_rs)
    qd = (qbuf, qd_ss, qd_rs)
    loads[0].wait()
    loads[1].wait()
    gather_start(*og)

    loads[3].wait()
    loads[4].wait()
    lane14 = lax.broadcasted_iota(jnp.int32, (14, 128), 1)
    for col in range(width // 128):
        column = jnp.where(
            lane14 < 64,
            jnp.broadcast_to(osc[:, 2 * col : 2 * col + 1], (14, 128)),
            jnp.broadcast_to(osc[:, 2 * col + 1 : 2 * col + 2], (14, 128)),
        )
        at = pl.ds(col * 128, 128)
        scale[:, at] = (bsc[:, at] + 1).astype(F32) / 256.0 * column
    loads[2].wait()

    def dequant(b, _):
        rows = pl.ds(pl.multiple_of(b * 64, 64), 64)
        w[rows, :] = (lookup(codes[rows, :]) * scale[pl.ds(b, 1), :]).astype(BF16)
        return 0

    lax.fori_loop(0, 8, dequant, 0)
    gather_more(*og)
    lax.fori_loop(8, 14, dequant, 0)


    loads[7].wait()
    mine = jnp.zeros((16, 112), F32)
    for j in range(8):
        mine = jnp.where(tn == j, au[:, j * 112 : (j + 1) * 112].astype(F32), mine)
    auj[...] = mine.astype(BF16)
    gb[...] = jnp.zeros_like(gb)
    fac[...] = jnp.zeros_like(fac)
    loads[8].wait()


    def project():
        proj[dp] = lax.dot_general(ad[...], xs[...], NT, preferred_element_type=F32).astype(BF16)

    for i in (5, 6, 9, 10, 11):
        loads[i].wait()

    def proj_copy(o, to):
        return pltpu.make_async_remote_copy(
            src_ref=proj.at[dp], dst_ref=proj.at[dp], send_sem=p_ss.at[o], recv_sem=p_rs.at[o],
            device_id={"dp": ((dp + o) & 31)}, device_id_type=MESH,
        )

    def proj_send(o, _):
        proj_copy(o, None).start()
        return 0

    def core_copy(p):
        return pltpu.make_async_remote_copy(
            src_ref=csend.at[p], dst_ref=crecv.at[p], send_sem=c_ss.at[p], recv_sem=c_rs.at[p],
            device_id={"tensor": zh * 2 + 1 - c}, device_id_type=MESH,
        )

    def ring_copy(p, d, i):
        step = 1 if d == 0 else 3
        return pltpu.make_async_remote_copy(
            src_ref=rsend.at[p, d, i], dst_ref=rrecv.at[p, d, i], send_sem=r_ss.at[p, d, i],
            recv_sem=r_rs.at[p, d, i],
            device_id={"tensor": ((zh + step) & 3) * 2 + c}, device_id_type=MESH,
        )

    def ring_target(d, i):
        return (zh + (3 - i if d == 0 else i + 1)) & 3

    def multiply(p):
        parts = piece_parts(p)
        rows = jnp.concatenate(
            [buf[k, pair_of(k, a, b), half_of(w)] for k in range(2) for a, b, w in parts], axis=0
        )
        slot = (p & (SLOTS - 1))
        prod[slot] = lax.dot_general(w[...], rows, NT, preferred_element_type=F32).reshape(8, 112, 256)
        for k in range(4):
            csend[p, k] = prod[slot, 2 * k + 1 - c].astype(BF16)
        core_copy(p).start()

    def chip_sum(p, d, k):
        at = slice(d * 128, (d + 1) * 128)
        return prod[(p & (SLOTS - 1)), 2 * k + c, :, at] + crecv[p, k, :, at].astype(F32)

    def core_add(p):
        core_copy(p).wait_recv()
        for d in range(2):
            rsend[p, d, 0] = chip_sum(p, d, ring_target(d, 0)).astype(BF16)
            ring_copy(p, d, 0).start()

    def ring_add(p, i):
        for d in range(2):
            ring_copy(p, d, i - 1).wait_recv()
            part = chip_sum(p, d, ring_target(d, i))
            rsend[p, d, i] = (part + rrecv[p, d, i - 1].astype(F32)).astype(BF16)
            ring_copy(p, d, i).start()

    lane16 = lax.broadcasted_iota(jnp.int32, (16, 128), 1)
    low = lane16 < 64
    low112 = lax.broadcasted_iota(jnp.int32, (112, 128), 1) < 64

    def example_at(pair, half):
        return (pair >> 2) * 8 + half * 4 + (pair & 3)

    def finish(p):
        parts = piece_parts(p)
        for d in range(2):
            ring_copy(p, d, 2).wait_recv()
        sums = []
        for d in range(2):
            hidden = chip_sum(p, d, zh) + rrecv[p, d, 2].astype(F32)
            e0, e1 = [example_at(pair_of(d, a, b), half_of(w)) for a, b, w in parts]
            g0, g1 = [gate[:, pl.ds(pl.multiple_of(e * 128, 128), 128)].astype(F32) for e in (e0, e1)]
            p0, p1 = proj[e0].astype(F32), proj[e1].astype(F32)
            if d == 0:
                g1 = pltpu.roll(g1, 64, 1)
                p1 = pltpu.roll(p1, 64, 1)
            else:
                g0 = pltpu.roll(g0, 64, 1)
                p0 = pltpu.roll(p0, 64, 1)
            up = (hidden * jnp.where(low112, g0, g1)).astype(BF16)
            both = jnp.concatenate([jnp.where(low, p0, 0.0), jnp.where(low, 0.0, p1)], axis=0).astype(BF16)
            ft = lax.dot_general(auj[...], up, NN, preferred_element_type=F32)
            grad = lax.dot_general(both, up, NT, preferred_element_type=F32)
            sums.append((e0, e1, ft, grad))
        for d, (e0, e1, ft, grad) in enumerate(sums):
            turned = pltpu.roll(ft, 64, 1)
            if d == 0:
                fac[e0] += jnp.where(low, ft, 0.0)
                fac[e1] += jnp.where(low, turned, 0.0)
            else:
                fac[e0] += jnp.where(low, 0.0, turned)
                fac[e1] += jnp.where(low, 0.0, ft)
            gb[pl.ds(pl.multiple_of(e0 * 16, 16), 16), :] += grad[0:16]
            gb[pl.ds(pl.multiple_of(e1 * 16, 16), 16), :] += grad[16:32]

    def t1_copy(o):
        return pltpu.make_async_remote_copy(
            src_ref=fac.at[((dp + o) & 31)], dst_ref=t1.at[o], send_sem=t1_ss.at[o], recv_sem=t1_rs.at[o],
            device_id={"dp": ((dp + o) & 31)}, device_id_type=MESH,
        )

    def t1b_copy(o, rows=sbs):
        return pltpu.make_async_remote_copy(
            src_ref=rows.at[((dp + o) & 31)], dst_ref=t1b.at[o], send_sem=t1b_ss.at[o], recv_sem=t1b_rs.at[o],
            device_id={"dp": ((dp + o) & 31)}, device_id_type=MESH,
        )

    def send_each(copy, places):
        for u, v, w in places:
            e = example_at(pair_at(0, u, v), half_of(w))
            if u == v == 0:

                @pl.when(half_of(w) != l)
                def _(e=e):
                    copy((e + 32 - dp) & 31).start()
            else:
                copy((e + 32 - dp) & 31).start()

    def hand_over(p):
        for i in range(PIECES):
            if complete_at(i):

                @pl.when(p == i)
                def _(i=i):
                    send_each(t1_copy, complete_at(i))

    def score_up():
        score_b = jnp.zeros((32, 128), F32)
        for r in range(16):
            part = gb[pl.ds(r, 32, stride=16), :].astype(BF16)
            score_b += lax.dot_general(part, qu[r], NN, preferred_element_type=F32)
        return jnp.broadcast_to(score_b[:, None, :], (32, 8, 128))

    def meet(n, _):
        xd = xs[:, pl.ds(pl.multiple_of(tn * width, 128), width)]
        a, b = [pick(n, {i: offset(place[j]) for i, place in enumerate(MEET)}) for j in range(2)]
        pairs = [pair_of(k, a, b) for k in range(2)]
        rows = jnp.concatenate([qbuf[k, pairs[k]].reshape(64, width) for k in range(2)], axis=0)
        part = lax.dot_general(rows, xd, NT, preferred_element_type=F32).reshape(2, 2, 32, 128)
        for k in range(2):
            for half in range(2):
                start = example_at(pairs[k], half) * 64 + k * 32
                mt[pl.ds(pl.multiple_of(start, 32), 32), :] = part[k, half]
        return 0

    def proj_drain(o, _):
        proj_copy(o, None).wait_send()
        return 0

    def met(s):
        count = 0
        for at, n in MET.items():
            count = jnp.where(s > at, n, count)
        return count

    def iteration(s, _):
        @pl.when((s >= 1 + LAG) & (s - 1 - LAG < PIECES))
        def _():
            ring_add(s - 1 - LAG, 1)

        @pl.when((s >= 1 + 2 * LAG) & (s - 1 - 2 * LAG < PIECES))
        def _():
            ring_add(s - 1 - 2 * LAG, 2)

        @pl.when((s >= 1) & (s - 1 < PIECES))
        def _():
            core_add(s - 1)

        @pl.when(s < 4)
        def _():
            for at, actions in OG_BEFORE.items():

                @pl.when(s == at)
                def _(actions=actions):
                    gather_do(og, actions)

        @pl.when(s < PIECES)
        def _():
            multiply(s)

        @pl.when(s == 1)
        def _():
            project()

        @pl.when((s >= 2) & (s < 6))
        def _():
            lax.fori_loop(jnp.maximum(8 * s - 16, 1), 8 * s - 8, proj_send, 0)

        for low_s in range(0, PIECES + STAGES, 6):

            @pl.when((s >= low_s) & (s < low_s + 6))
            def _(low_s=low_s):
                for at in range(low_s, low_s + 6):
                    if at in OG_AFTER or at in QD_AFTER:

                        @pl.when(s == at)
                        def _(at=at):
                            gather_do(og, OG_AFTER.get(at, ()))
                            gather_do(qd, QD_AFTER.get(at, ()))

        @pl.when(s == STAGES)
        def _():
            def proj_wait(o, _):
                proj_copy(o, None).wait_recv()
                return 0

            lax.fori_loop(1, 32, proj_wait, 0)

        @pl.when(s >= STAGES)
        def _():
            finish(s - STAGES)
            hand_over(s - STAGES)
            core_copy(s - STAGES).wait_send()
            for d in range(2):
                for i in range(3):
                    ring_copy(s - STAGES, d, i).wait_send()

        @pl.when(s == 10)
        def _():
            lax.fori_loop(1, 32, proj_drain, 0)

        @pl.when(s == 17)
        def _():
            gather_drain(*og)

        lax.fori_loop(met(s), met(s + 1), meet, 0)

        @pl.when(s == STAGES + EARLY)
        def _():
            sbs[...] = score_up()
            send_each(t1b_copy, [e for i in range(EARLY + 1) for e in complete_at(i)])

        return 0

    lax.fori_loop(0, PIECES + STAGES, iteration, 0)

    def t1_take(o, total):
        t1_copy(o).wait_recv()
        return total + t1[o]

    def t2_copy(o):
        return pltpu.make_async_remote_copy(
            src_ref=t2s, dst_ref=t2.at[o], send_sem=t2_ss.at[o], recv_sem=t2_rs.at[o],
            device_id={"tensor": ((tn + o) & 7)}, device_id_type=MESH,
        )

    t2s[...] = lax.fori_loop(1, 32, t1_take, fac[dp])
    for o in range(1, 8):
        t2_copy(o).start()

    late = [e for i in range(EARLY + 1, PIECES) for e in complete_at(i)]
    sbl[...] = score_up()
    send_each(lambda o: t1b_copy(o, sbl), late)

    factors = t2s[...]
    for o in range(1, 8):
        t2_copy(o).wait_recv()
        factors += t2[o]

    def t3_copy(o):
        return pltpu.make_async_remote_copy(
            src_ref=t3s, dst_ref=t3.at[o], send_sem=t3_ss.at[o], recv_sem=t3_rs.at[o],
            device_id={"tensor": ((tn + o) & 7)}, device_id_type=MESH,
        )

    def weigh(i, _):
        rows = mt[pl.ds(pl.multiple_of(i * 128, 128), 128), :].reshape(8, 16, 128)
        acc[pl.ds(pl.multiple_of(i * 8, 8), 8), :] = jnp.sum(rows * factors[None], axis=1)
        return 0

    lax.fori_loop(0, 16, weigh, 0)
    score_a = lax.dot_general(
        jnp.ones((8, 128), F32), acc[...], NT, precision=lax.Precision.HIGHEST, preferred_element_type=F32
    )

    def t1b_take(o, total):
        t1b_copy(o).wait_recv()
        return total + t1b[o]

    t3s[...] = lax.fori_loop(1, 32, t1b_take, sbs[dp] + score_a)
    for o in range(1, 8):
        t3_copy(o).start()
    gather_drain(*qd)

    def t1_drain(o, _):
        t1_copy(o).wait_send()
        t1b_copy(o).wait_send()
        return 0

    lax.fori_loop(1, 32, t1_drain, 0)
    for o in range(1, 8):
        t2_copy(o).wait_send()
    scores = t3s[...]
    for o in range(1, 8):
        t3_copy(o).wait_recv()
        scores += t3[o]
    out = jnp.zeros((1, 16), F32)
    for j in range(8):
        out = jnp.where(tn == j, scores[0:1, j * 16 : (j + 1) * 16], out)
    out_ref[...] = out
    for o in range(1, 8):
        t3_copy(o).wait_send()


def shards(x, og, gate, codes, bsc, osc, ad, au, qd, qu):
    qd = qd.reshape(64, 1024)
    gate = gate.T
    qu = qu.transpose(1, 2, 0)
    dma = pltpu.SemaphoreType.DMA
    vmem = pltpu.VMEM
    return pl.pallas_call(
        kernel,
        out_shape=jax.ShapeDtypeStruct((1, 16), F32),
        in_specs=[ANY] * 10,
        out_specs=pl.BlockSpec(memory_space=pltpu.VMEM),
        scratch_shapes=[
            vmem((2, 16, 2, 64, 1024), BF16),
            vmem((2, 16, 2, 32, 1024), BF16),
            vmem((896, 1024), jnp.int32),
            vmem((14, 1024), jnp.int32),
            vmem((14, 16), F32),
            vmem((14, 1024), F32),
            vmem((896, 1024), BF16),
            vmem((128, 8192), BF16),
            vmem((16, 8192), BF16),
            vmem((16, 896), BF16),
            vmem((16, 112), BF16),
            vmem((112, 4096), BF16),
            vmem((16, 112, 128), BF16),
            vmem((SLOTS, 8, 112, 256), F32),
            vmem((PIECES, 4, 112, 256), BF16),
            vmem((PIECES, 4, 112, 256), BF16),
            vmem((PIECES, 2, 3, 112, 128), BF16),
            vmem((PIECES, 2, 3, 112, 128), BF16),
            vmem((32, 16, 128), BF16),
            vmem((512, 112), F32),
            vmem((32, 16, 128), F32),
            vmem((32, 16, 128), F32),
            vmem((16, 128), F32),
            vmem((8, 16, 128), F32),
            vmem((32, 8, 128), F32),
            vmem((32, 8, 128), F32),
            vmem((32, 8, 128), F32),
            vmem((2048, 128), F32),
            vmem((128, 128), F32),
            vmem((8, 128), F32),
            vmem((8, 8, 128), F32),
            dma((12,)),
            dma((2, 4, 4, 2)),
            dma((2, 4, 4, 2)),
            dma((2, 4, 4, 2)),
            dma((2, 4, 4, 2)),
            dma((PIECES,)),
            dma((PIECES,)),
            dma((PIECES, 2, 3)),
            dma((PIECES, 2, 3)),
            dma((32,)),
            dma((32,)),
            dma((32,)),
            dma((32,)),
            dma((32,)),
            dma((32,)),
            dma((8,)),
            dma((8,)),
            dma((8,)),
            dma((8,)),
        ],
        compiler_params=pltpu.CompilerParams(
            collective_id=0, has_side_effects=True, vmem_limit_bytes=60 * 1024 * 1024
        ),
        name="influence",
    )(x, og, gate, codes, bsc, osc, ad, au, qd, qu)


def solution(mesh):
    in_specs = (
        P("dp", None),
        P("dp", "tensor"),
        P(None, ("dp", "tensor")),
        P("dp", "tensor"),
        P("dp", "tensor"),
        P("dp", "tensor"),
        P(),
        P(None, "dp"),
        P("dp", None, "tensor"),
        P(None, None, ("dp", "tensor")),
    )
    return jax.shard_map(shards, mesh=mesh, in_specs=in_specs, out_specs=P("dp", "tensor"), check_vma=False)
```

```python
import jax
import jax.numpy as jnp
from jax import lax
from jax.experimental import pallas as pl
from jax.experimental.pallas import tpu as pltpu
from jax.sharding import PartitionSpec as P

MESH = pl.DeviceIdType.MESH
F32 = jnp.float32
BF16 = jnp.bfloat16
NT = (((1,), (1,)), ((), ()))
NN = (((1,), (0,)), ((), ()))
ANY = pl.BlockSpec(memory_space=pl.ANY)

PIECES = 16
SLOTS = 8
LAG = 2
STAGES = 1 + 3 * LAG

LEVELS = (
    -1.0,
    -0.6961928009986877,
    -0.5250730514526367,
    -0.39491748809814453,
    -0.28444138169288635,
    -0.18477343022823334,
    -0.09105003625154495,
    0.0,
    0.07958029955625534,
    0.16093020141124725,
    0.24611230194568634,
    0.33791524171829224,
    0.44070982933044434,
    0.5626170039176941,
    0.7229568362236023,
    1.0,
)


def lookup(codes):
    values = [jnp.full(codes.shape, level, F32) for level in LEVELS]
    for bit in range(4):
        odd = (codes & (1 << bit)) != 0
        values = [jnp.where(odd, values[i + 1], values[i]) for i in range(0, len(values), 2)]
    return values[0]


def offset(k):
    return k + k // 2 - 2 * (k // 3)


OWN, OTHER = 2, 3
WHOLE = [(0, 0), (3, 0), (0, 3), (1, 1), (1, 2), (2, 1), (2, 2), (1, 3), (3, 1), (3, 2), (2, 3), (3, 3)]
WHOLE = [((u, v, 0), (u, v, 1)) for u, v in WHOLE]
ORDER = [
    ((1, 0, OWN), (2, 0, OWN)),
    WHOLE[0],
    ((0, 1, OWN), (0, 2, OWN)),
    ((1, 0, OTHER), (2, 0, OTHER)),
    ((0, 1, OTHER), (0, 2, OTHER)),
] + WHOLE[1:]
PLACE = {part: i for i, parts in enumerate(ORDER) for part in parts}


def complete_at(p):
    return [(u, v, w) for (u, v, w), i in PLACE.items() if max(i, PLACE[v, u, w]) == p]


def piece_parts(n):
    found = []
    for side in range(2):
        code = pick(n, {i: offset(u) + 4 * offset(v) + 16 * w for i, (u, v, w) in enumerate(parts[side] for parts in ORDER)})
        found.append((code & 3, (code >> 2) & 3, code >> 4))
    return found


def pick(n, table):
    value = 0
    for i, entry in table.items():
        value = jnp.where(n == i, entry, value)
    return value


def takes(*places):
    return [("take", u, v, w) for u, v in places for w in (OWN, OTHER)]


OG_BEFORE = {
    0: [("take", 1, 0, OWN), ("take", 2, 0, OWN)],
    1: [("take", 0, 0, OTHER)],
    3: [("take", 1, 0, OTHER), ("take", 2, 0, OTHER)],
}
OG_AFTER = {
    1: [("take", 0, 1, OWN), ("take", 0, 2, OWN)],
    3: [("take", 0, 1, OTHER), ("take", 0, 2, OTHER), ("second", 1)],
    4: takes((3, 0)),
    5: takes((0, 3)) + [("second", 2)],
    6: [("whole", 1, 1), ("whole", 1, 2), ("second", 3)],
    8: [("whole", 2, 1), ("whole", 2, 2)],
    10: takes((1, 3)),
    11: [("whole", 3, 1), ("whole", 3, 2)],
    12: takes((2, 3)),
    14: takes((3, 3)),
}
QD_AFTER = {
    10: [("start",), ("more",)],
    11: [("take", 0, 0, OTHER)],
    13: takes((1, 0), (2, 0), (0, 1), (0, 2)) + [("second", 1), ("second", 2)],
    14: takes((3, 0), (0, 3)) + [("second", 3)],
    15: [("whole", 1, 1), ("whole", 1, 2)],
    16: [("whole", 2, 1), ("whole", 2, 2)],
    18: [("whole", 3, 1), ("whole", 3, 2)] + takes((1, 3)),
    19: takes((2, 3)),
    20: takes((3, 3)),
}
MEET = [(0, 0), (1, 0), (2, 0), (0, 1), (0, 2), (3, 0), (0, 3), (1, 1), (1, 2), (2, 1), (2, 2), (3, 1), (3, 2), (1, 3), (2, 3), (3, 3)]
MET = {11: 1, 13: 5, 14: 7, 15: 9, 16: 11, 18: 14, 19: 15, 20: 16}
EARLY = 12


def kernel(
    x_hbm, og_hbm, gate_hbm, codes_hbm, bsc_hbm, osc_hbm, ad_hbm, au_hbm, qd_hbm, qu_hbm,
    out_ref,
    buf, qbuf, codes, bsc, osc, scale, w, xs, ad, au, auj, gate, qu,
    prod, csend, crecv, rsend, rrecv, proj, gb, fac, t1, t2s, t2, sbs, sbl, t1b, mt, acc, t3s, t3,
    lsem, og_ss, og_rs, qd_ss, qd_rs, c_ss, c_rs, r_ss, r_rs, p_ss, p_rs, t1_ss, t1_rs, t1b_ss, t1b_rs, t2_ss, t2_rs, t3_ss, t3_rs,
):
    dp = lax.axis_index("dp")
    tn = lax.axis_index("tensor")
    y, l, x = dp & 3, (dp >> 2) & 1, dp >> 3
    zh, c = tn >> 1, tn & 1

    width = og_hbm.shape[1]
    here = x * 4 + y
    loads = [
        (og_hbm.at[pl.ds(0, 64)], buf.at[0, here, l]),
        (og_hbm.at[pl.ds(64, 64)], buf.at[1, here, l]),
        (codes_hbm, codes),
        (bsc_hbm, bsc),
        (osc_hbm, osc),
        (x_hbm, xs),
        (ad_hbm, ad),
        (au_hbm, au),
        (gate_hbm, gate),
        (qd_hbm.at[pl.ds(0, 32)], qbuf.at[0, here, l]),
        (qd_hbm.at[pl.ds(32, 32)], qbuf.at[1, here, l]),
        (qu_hbm, qu),
    ]
    loads = [pltpu.make_async_copy(a, b, lsem.at[i]) for i, (a, b) in enumerate(loads)]
    for load in loads:
        load.start()

    barrier = pltpu.get_barrier_semaphore()

    def greet_dp(o, _):
        pl.semaphore_signal(barrier, 1, device_id={"dp": ((dp + o) & 31)}, device_id_type=MESH)
        return 0

    def greet_tn(o, _):
        pl.semaphore_signal(barrier, 1, device_id={"tensor": ((tn + o) & 7)}, device_id_type=MESH)
        return 0

    lax.fori_loop(1, 32, greet_dp, 0)
    lax.fori_loop(1, 8, greet_tn, 0)
    pl.semaphore_wait(barrier, 38)

    def pair_of(k, a, b):
        if k == 1:
            a, b = b, a
        return ((x + a) & 3) * 4 + ((y + b) & 3)

    def pair_at(k, u, v):
        return pair_of(k, offset(u), offset(v))

    def near(k, first, step):
        along_x = first == (k == 0)
        if along_x:
            return {"dp": (((x + step) & 3) * 2 + l) * 4 + y}
        return {"dp": (x * 2 + l) * 4 + ((y + step) & 3)}

    def piece_copy(data, ss, rs, k, u, v, half, ur, vr, target):
        ref = data.at[k, pair_at(k, u, v)]
        sem = 0 if half is None else half
        ref = ref if half is None else ref.at[half]
        return pltpu.make_async_remote_copy(
            src_ref=ref, dst_ref=ref, send_sem=ss.at[k, ur, vr, sem], recv_sem=rs.at[k, ur, vr, sem],
            device_id=target, device_id_type=MESH,
        )

    partner = {"dp": (x * 2 + 1 - l) * 4 + y}

    def half_of(w):
        if isinstance(w, int):
            return w if w < 2 else l if w == OWN else 1 - l
        return jnp.where(w < 2, w, jnp.where(w == OWN, l, 1 - l))

    def gather_first(data, ss, rs, k, half):
        piece_copy(data, ss, rs, k, 0, 0, half, 2, 0, near(k, True, 1)).start()
        piece_copy(data, ss, rs, k, 0, 0, half, 1, 0, near(k, True, 3)).start()

    def gather_more(data, ss, rs, half=None):
        half = l if half is None else half
        for k in range(2):
            piece_copy(data, ss, rs, k, 0, 0, half, 0, 2, near(k, False, 1)).start()
            piece_copy(data, ss, rs, k, 0, 0, half, 0, 1, near(k, False, 3)).start()

    def gather_start(data, ss, rs):
        for k in range(2):
            piece_copy(data, ss, rs, k, 0, 0, l, 0, 0, partner).start()
            gather_first(data, ss, rs, k, l)

    def gather_second(data, ss, rs, u):
        for k in range(2):
            piece_copy(data, ss, rs, k, u, 0, None, u, 2, near(k, False, 1)).start()
            piece_copy(data, ss, rs, k, u, 0, None, u, 1, near(k, False, 3)).start()

    def gather_take(data, ss, rs, u, v, w):
        half = half_of(w)
        for k in range(2):
            piece_copy(data, ss, rs, k, u, v, half, u, v, partner).wait_recv()
            if (u, v) == (0, 0):
                gather_first(data, ss, rs, k, half)
            if (u, v) in ((1, 0), (2, 0), (0, 1), (0, 2)):
                step, at = (3, 1) if 1 in (u, v) else (1, 0)
                ur, vr = (3, 0) if v == 0 else (0, 3)

                @pl.when(half == at)
                def _(k=k, step=step, at=at, ur=ur, vr=vr):
                    piece_copy(data, ss, rs, k, u, v, at, ur, vr, near(k, v == 0, step)).start()
        if (u, v) == (0, 0):
            gather_more(data, ss, rs, half)

    def gather_whole(data, ss, rs, u, v):
        for k in range(2):
            piece_copy(data, ss, rs, k, u, v, None, u, v, partner).wait_recv()
            step, at = (3, 1) if v == 1 else (1, 0)
            piece_copy(data, ss, rs, k, u, v, at, u, 3, near(k, False, step)).start()

    def gather_do(gather, actions):
        for action in actions:
            act = {
                "start": gather_start, "more": gather_more, "second": gather_second,
                "take": gather_take, "whole": gather_whole,
            }[action[0]]
            act(*gather, *action[1:])

    def gather_drain(data, ss, rs):
        for k in range(2):
            for u in range(4):
                for v in range(4):
                    pieces = (l,) if u == v == 0 else (0, 1) if u == 0 or v in (0, 3) else (None,)
                    for half in pieces:
                        piece_copy(data, ss, rs, k, 0, 0, half, u, v, partner).wait_send()

    og = (buf, og_ss, og_rs)
    qd = (qbuf, qd_ss, qd_rs)
    loads[0].wait()
    loads[1].wait()
    gather_start(*og)

    loads[3].wait()
    loads[4].wait()
    lane14 = lax.broadcasted_iota(jnp.int32, (14, 128), 1)
    for col in range(width // 128):
        column = jnp.where(
            lane14 < 64,
            jnp.broadcast_to(osc[:, 2 * col : 2 * col + 1], (14, 128)),
            jnp.broadcast_to(osc[:, 2 * col + 1 : 2 * col + 2], (14, 128)),
        )
        at = pl.ds(col * 128, 128)
        scale[:, at] = (bsc[:, at] + 1).astype(F32) / 256.0 * column
    loads[2].wait()

    def dequant(b, _):
        rows = pl.ds(pl.multiple_of(b * 64, 64), 64)
        w[rows, :] = (lookup(codes[rows, :]) * scale[pl.ds(b, 1), :]).astype(BF16)
        return 0

    lax.fori_loop(0, 8, dequant, 0)
    gather_more(*og)
    lax.fori_loop(8, 14, dequant, 0)


    loads[7].wait()
    mine = jnp.zeros((16, 112), F32)
    for j in range(8):
        mine = jnp.where(tn == j, au[:, j * 112 : (j + 1) * 112].astype(F32), mine)
    auj[...] = mine.astype(BF16)
    gb[...] = jnp.zeros_like(gb)
    fac[...] = jnp.zeros_like(fac)
    loads[8].wait()


    def project():
        proj[dp] = lax.dot_general(ad[...], xs[...], NT, preferred_element_type=F32).astype(BF16)

    for i in (5, 6, 9, 10, 11):
        loads[i].wait()

    def proj_copy(o, to):
        return pltpu.make_async_remote_copy(
            src_ref=proj.at[dp], dst_ref=proj.at[dp], send_sem=p_ss.at[o], recv_sem=p_rs.at[o],
            device_id={"dp": ((dp + o) & 31)}, device_id_type=MESH,
        )

    def proj_send(o, _):
        proj_copy(o, None).start()
        return 0

    def core_copy(p):
        return pltpu.make_async_remote_copy(
            src_ref=csend.at[p], dst_ref=crecv.at[p], send_sem=c_ss.at[p], recv_sem=c_rs.at[p],
            device_id={"tensor": zh * 2 + 1 - c}, device_id_type=MESH,
        )

    def ring_copy(p, d, i):
        step = 1 if d == 0 else 3
        return pltpu.make_async_remote_copy(
            src_ref=rsend.at[p, d, i], dst_ref=rrecv.at[p, d, i], send_sem=r_ss.at[p, d, i],
            recv_sem=r_rs.at[p, d, i],
            device_id={"tensor": ((zh + step) & 3) * 2 + c}, device_id_type=MESH,
        )

    def ring_target(d, i):
        return (zh + (3 - i if d == 0 else i + 1)) & 3

    def multiply(p):
        parts = piece_parts(p)
        rows = jnp.concatenate(
            [buf[k, pair_of(k, a, b), half_of(w)] for k in range(2) for a, b, w in parts], axis=0
        )
        slot = (p & (SLOTS - 1))
        prod[slot] = lax.dot_general(w[...], rows, NT, preferred_element_type=F32).reshape(8, 112, 256)
        for k in range(4):
            csend[p, k] = prod[slot, 2 * k + 1 - c].astype(BF16)
        core_copy(p).start()

    def chip_sum(p, d, k):
        at = slice(d * 128, (d + 1) * 128)
        return prod[(p & (SLOTS - 1)), 2 * k + c, :, at] + crecv[p, k, :, at].astype(F32)

    def core_add(p):
        core_copy(p).wait_recv()
        for d in range(2):
            rsend[p, d, 0] = chip_sum(p, d, ring_target(d, 0)).astype(BF16)
            ring_copy(p, d, 0).start()

    def ring_add(p, i):
        for d in range(2):
            ring_copy(p, d, i - 1).wait_recv()
            part = chip_sum(p, d, ring_target(d, i))
            rsend[p, d, i] = (part + rrecv[p, d, i - 1].astype(F32)).astype(BF16)
            ring_copy(p, d, i).start()

    lane16 = lax.broadcasted_iota(jnp.int32, (16, 128), 1)
    low = lane16 < 64
    low112 = lax.broadcasted_iota(jnp.int32, (112, 128), 1) < 64

    def example_at(pair, half):
        return (pair >> 2) * 8 + half * 4 + (pair & 3)

    def finish(p):
        parts = piece_parts(p)
        for d in range(2):
            ring_copy(p, d, 2).wait_recv()
        sums = []
        for d in range(2):
            hidden = chip_sum(p, d, zh) + rrecv[p, d, 2].astype(F32)
            e0, e1 = [example_at(pair_of(d, a, b), half_of(w)) for a, b, w in parts]
            g0, g1 = [gate[:, pl.ds(pl.multiple_of(e * 128, 128), 128)].astype(F32) for e in (e0, e1)]
            p0, p1 = proj[e0].astype(F32), proj[e1].astype(F32)
            if d == 0:
                g1 = pltpu.roll(g1, 64, 1)
                p1 = pltpu.roll(p1, 64, 1)
            else:
                g0 = pltpu.roll(g0, 64, 1)
                p0 = pltpu.roll(p0, 64, 1)
            up = (hidden * jnp.where(low112, g0, g1)).astype(BF16)
            both = jnp.concatenate([jnp.where(low, p0, 0.0), jnp.where(low, 0.0, p1)], axis=0).astype(BF16)
            ft = lax.dot_general(auj[...], up, NN, preferred_element_type=F32)
            grad = lax.dot_general(both, up, NT, preferred_element_type=F32)
            sums.append((e0, e1, ft, grad))
        for d, (e0, e1, ft, grad) in enumerate(sums):
            turned = pltpu.roll(ft, 64, 1)
            if d == 0:
                fac[e0] += jnp.where(low, ft, 0.0)
                fac[e1] += jnp.where(low, turned, 0.0)
            else:
                fac[e0] += jnp.where(low, 0.0, turned)
                fac[e1] += jnp.where(low, 0.0, ft)
            gb[pl.ds(pl.multiple_of(e0 * 16, 16), 16), :] += grad[0:16]
            gb[pl.ds(pl.multiple_of(e1 * 16, 16), 16), :] += grad[16:32]

    def t1_copy(o):
        return pltpu.make_async_remote_copy(
            src_ref=fac.at[((dp + o) & 31)], dst_ref=t1.at[o], send_sem=t1_ss.at[o], recv_sem=t1_rs.at[o],
            device_id={"dp": ((dp + o) & 31)}, device_id_type=MESH,
        )

    def t1b_copy(o, rows=sbs):
        return pltpu.make_async_remote_copy(
            src_ref=rows.at[((dp + o) & 31)], dst_ref=t1b.at[o], send_sem=t1b_ss.at[o], recv_sem=t1b_rs.at[o],
            device_id={"dp": ((dp + o) & 31)}, device_id_type=MESH,
        )

    def send_each(copy, places):
        for u, v, w in places:
            e = example_at(pair_at(0, u, v), half_of(w))
            if u == v == 0:

                @pl.when(half_of(w) != l)
                def _(e=e):
                    copy((e + 32 - dp) & 31).start()
            else:
                copy((e + 32 - dp) & 31).start()

    def hand_over(p):
        for i in range(PIECES):
            if complete_at(i):

                @pl.when(p == i)
                def _(i=i):
                    send_each(t1_copy, complete_at(i))

    def score_up():
        score_b = jnp.zeros((32, 128), F32)
        for r in range(16):
            part = gb[pl.ds(r, 32, stride=16), :].astype(BF16)
            score_b += lax.dot_general(part, qu[r], NN, preferred_element_type=F32)
        return jnp.broadcast_to(score_b[:, None, :], (32, 8, 128))

    def meet(n, _):
        xd = xs[:, pl.ds(pl.multiple_of(tn * width, 128), width)]
        a, b = [pick(n, {i: offset(place[j]) for i, place in enumerate(MEET)}) for j in range(2)]
        pairs = [pair_of(k, a, b) for k in range(2)]
        rows = jnp.concatenate([qbuf[k, pairs[k]].reshape(64, width) for k in range(2)], axis=0)
        part = lax.dot_general(rows, xd, NT, preferred_element_type=F32).reshape(2, 2, 32, 128)
        for k in range(2):
            for half in range(2):
                start = example_at(pairs[k], half) * 64 + k * 32
                mt[pl.ds(pl.multiple_of(start, 32), 32), :] = part[k, half]
        return 0

    def proj_drain(o, _):
        proj_copy(o, None).wait_send()
        return 0

    def met(s):
        count = 0
        for at, n in MET.items():
            count = jnp.where(s > at, n, count)
        return count

    def iteration(s, _):
        @pl.when((s >= 1 + LAG) & (s - 1 - LAG < PIECES))
        def _():
            ring_add(s - 1 - LAG, 1)

        @pl.when((s >= 1 + 2 * LAG) & (s - 1 - 2 * LAG < PIECES))
        def _():
            ring_add(s - 1 - 2 * LAG, 2)

        @pl.when((s >= 1) & (s - 1 < PIECES))
        def _():
            core_add(s - 1)

        @pl.when(s < 4)
        def _():
            for at, actions in OG_BEFORE.items():

                @pl.when(s == at)
                def _(actions=actions):
                    gather_do(og, actions)

        @pl.when(s < PIECES)
        def _():
            multiply(s)

        @pl.when(s == 1)
        def _():
            project()

        @pl.when((s >= 2) & (s < 6))
        def _():
            lax.fori_loop(jnp.maximum(8 * s - 16, 1), 8 * s - 8, proj_send, 0)

        for low_s in range(0, PIECES + STAGES, 6):

            @pl.when((s >= low_s) & (s < low_s + 6))
            def _(low_s=low_s):
                for at in range(low_s, low_s + 6):
                    if at in OG_AFTER or at in QD_AFTER:

                        @pl.when(s == at)
                        def _(at=at):
                            gather_do(og, OG_AFTER.get(at, ()))
                            gather_do(qd, QD_AFTER.get(at, ()))

        @pl.when(s == STAGES)
        def _():
            def proj_wait(o, _):
                proj_copy(o, None).wait_recv()
                return 0

            lax.fori_loop(1, 32, proj_wait, 0)

        @pl.when(s >= STAGES)
        def _():
            finish(s - STAGES)
            hand_over(s - STAGES)
            core_copy(s - STAGES).wait_send()
            for d in range(2):
                for i in range(3):
                    ring_copy(s - STAGES, d, i).wait_send()

        @pl.when(s == 10)
        def _():
            lax.fori_loop(1, 32, proj_drain, 0)

        @pl.when(s == 17)
        def _():
            gather_drain(*og)

        lax.fori_loop(met(s), met(s + 1), meet, 0)

        @pl.when(s == STAGES + EARLY)
        def _():
            sbs[...] = score_up()
            send_each(t1b_copy, [e for i in range(EARLY + 1) for e in complete_at(i)])

        return 0

    lax.fori_loop(0, PIECES + STAGES, iteration, 0)

    def t1_take(o, total):
        t1_copy(o).wait_recv()
        return total + t1[o]

    def t2_copy(o):
        return pltpu.make_async_remote_copy(
            src_ref=t2s, dst_ref=t2.at[o], send_sem=t2_ss.at[o], recv_sem=t2_rs.at[o],
            device_id={"tensor": ((tn + o) & 7)}, device_id_type=MESH,
        )

    t2s[...] = lax.fori_loop(1, 32, t1_take, fac[dp])
    for o in range(1, 8):
        t2_copy(o).start()

    late = [e for i in range(EARLY + 1, PIECES) for e in complete_at(i)]
    sbl[...] = score_up()
    send_each(lambda o: t1b_copy(o, sbl), late)

    factors = t2s[...]
    for o in range(1, 8):
        t2_copy(o).wait_recv()
        factors += t2[o]

    def t3_copy(o):
        return pltpu.make_async_remote_copy(
            src_ref=t3s, dst_ref=t3.at[o], send_sem=t3_ss.at[o], recv_sem=t3_rs.at[o],
            device_id={"tensor": ((tn + o) & 7)}, device_id_type=MESH,
        )

    def weigh(i, _):
        rows = mt[pl.ds(pl.multiple_of(i * 128, 128), 128), :].reshape(8, 16, 128)
        acc[pl.ds(pl.multiple_of(i * 8, 8), 8), :] = jnp.sum(rows * factors[None], axis=1)
        return 0

    lax.fori_loop(0, 16, weigh, 0)
    score_a = lax.dot_general(
        jnp.ones((8, 128), F32), acc[...], NT, precision=lax.Precision.HIGHEST, preferred_element_type=F32
    )

    def t1b_take(o, total):
        t1b_copy(o).wait_recv()
        return total + t1b[o]

    t3s[...] = lax.fori_loop(1, 32, t1b_take, sbs[dp] + score_a)
    for o in range(1, 8):
        t3_copy(o).start()
    gather_drain(*qd)

    def t1_drain(o, _):
        t1_copy(o).wait_send()
        t1b_copy(o).wait_send()
        return 0

    lax.fori_loop(1, 32, t1_drain, 0)
    for o in range(1, 8):
        t2_copy(o).wait_send()
    scores = t3s[...]
    for o in range(1, 8):
        t3_copy(o).wait_recv()
        scores += t3[o]
    out = jnp.zeros((1, 16), F32)
    for j in range(8):
        out = jnp.where(tn == j, scores[0:1, j * 16 : (j + 1) * 16], out)
    out_ref[...] = out
    for o in range(1, 8):
        t3_copy(o).wait_send()


def shards(x, og, gate, codes, bsc, osc, ad, au, qd, qu):
    qd = qd.reshape(64, 1024)
    gate = gate.T
    qu = qu.transpose(1, 2, 0)
    dma = pltpu.SemaphoreType.DMA
    vmem = pltpu.VMEM
    return pl.pallas_call(
        kernel,
        out_shape=jax.ShapeDtypeStruct((1, 16), F32),
        in_specs=[ANY] * 10,
        out_specs=pl.BlockSpec(memory_space=pltpu.VMEM),
        scratch_shapes=[
            vmem((2, 16, 2, 64, 1024), BF16),
            vmem((2, 16, 2, 32, 1024), BF16),
            vmem((896, 1024), jnp.int32),
            vmem((14, 1024), jnp.int32),
            vmem((14, 16), F32),
            vmem((14, 1024), F32),
            vmem((896, 1024), BF16),
            vmem((128, 8192), BF16),
            vmem((16, 8192), BF16),
            vmem((16, 896), BF16),
            vmem((16, 112), BF16),
            vmem((112, 4096), BF16),
            vmem((16, 112, 128), BF16),
            vmem((SLOTS, 8, 112, 256), F32),
            vmem((PIECES, 4, 112, 256), BF16),
            vmem((PIECES, 4, 112, 256), BF16),
            vmem((PIECES, 2, 3, 112, 128), BF16),
            vmem((PIECES, 2, 3, 112, 128), BF16),
            vmem((32, 16, 128), BF16),
            vmem((512, 112), F32),
            vmem((32, 16, 128), F32),
            vmem((32, 16, 128), F32),
            vmem((16, 128), F32),
            vmem((8, 16, 128), F32),
            vmem((32, 8, 128), F32),
            vmem((32, 8, 128), F32),
            vmem((32, 8, 128), F32),
            vmem((2048, 128), F32),
            vmem((128, 128), F32),
            vmem((8, 128), F32),
            vmem((8, 8, 128), F32),
            dma((12,)),
            dma((2, 4, 4, 2)),
            dma((2, 4, 4, 2)),
            dma((2, 4, 4, 2)),
            dma((2, 4, 4, 2)),
            dma((PIECES,)),
            dma((PIECES,)),
            dma((PIECES, 2, 3)),
            dma((PIECES, 2, 3)),
            dma((32,)),
            dma((32,)),
            dma((32,)),
            dma((32,)),
            dma((32,)),
            dma((32,)),
            dma((8,)),
            dma((8,)),
            dma((8,)),
            dma((8,)),
        ],
        compiler_params=pltpu.CompilerParams(
            collective_id=0, has_side_effects=True, vmem_limit_bytes=60 * 1024 * 1024
        ),
        name="influence",
    )(x, og, gate, codes, bsc, osc, ad, au, qd, qu)


def solution(mesh):
    in_specs = (
        P("dp", None),
        P("dp", "tensor"),
        P(None, ("dp", "tensor")),
        P("dp", "tensor"),
        P("dp", "tensor"),
        P("dp", "tensor"),
        P(),
        P(None, "dp"),
        P("dp", None, "tensor"),
        P(None, None, ("dp", "tensor")),
    )
    return jax.shard_map(shards, mesh=mesh, in_specs=in_specs, out_specs=P("dp", "tensor"), check_vma=False)
```
